32 devices in a mesh: dp: 8 (over z, y), tensor: 4 (over x, core).
Axes of the slice: x: 2, y: 2, z: 4, core: 2. Of those that a mesh axis runs over, the one named last changes fastest.
Arguments:
- tokens: bfloat16 [8192, 512], P('dp'), may hold values from -6 to 6
- memory: bfloat16 [8192, 512], P('dp'), may hold values from -6 to 6
- cotangent: bfloat16 [8192, 512], P('dp'), may hold values from -6 to 6
- lengths: int32 [16], P('dp'), may hold values from 1 to 512, 6144 in all
- breaks: int32 [16], P('dp'), may hold values from 1 to 501
- attn_in: float32 [6, 512, 512], P(None, 'dp', 'tensor'), may hold values from -0.25 to 0.25
- attn_out: float32 [2, 512, 512], P(None, 'dp', 'tensor'), may hold values from -3 to 3
- ffn_in: float32 [512, 2048], P('dp', 'tensor'), may hold values from -0.25 to 0.25
- ffn_out: float32 [512, 2048], P('dp', 'tensor'), may hold values from -0.125 to 0.125
- norms: float32 [6, 512], P(None, 'dp'), may hold values from -0.9 to 1.3, as said below
- attn_in_mom: float32 [6, 512, 512], P(None, 'dp', 'tensor'), may hold values from -256 to 256
- attn_out_mom: float32 [2, 512, 512], P(None, 'dp', 'tensor'), may hold values from -64 to 64
- ffn_in_mom: float32 [512, 2048], P('dp', 'tensor'), may hold values from -256 to 256
- ffn_out_mom: float32 [512, 2048], P('dp', 'tensor'), may hold values from -256 to 256
- norms_mom: float32 [6, 512], P(None, 'dp'), may hold values from -256 to 256
- attn_in_avg: float32 [6, 512, 512], P(None, 'dp', 'tensor'), may hold values from -0.25 to 0.25
- attn_out_avg: float32 [2, 512, 512], P(None, 'dp', 'tensor'), may hold values from -3 to 3
- ffn_in_avg: float32 [512, 2048], P('dp', 'tensor'), may hold values from -0.25 to 0.25
- ffn_out_avg: float32 [512, 2048], P('dp', 'tensor'), may hold values from -0.125 to 0.125
- norms_avg: float32 [6, 512], P(None, 'dp'), may hold values from 0.5 to 1.5
Outputs:
- block_out: bfloat16 [8192, 512], P('dp')
- tokens_grad: float32 [8192, 512], P('dp')
- attn_in_grad: float32 [6, 512, 512], P(None, 'dp', 'tensor')
- attn_in_mom_new: float32 [6, 512, 512], P(None, 'dp', 'tensor')
- attn_in_new: float32 [6, 512, 512], P(None, 'dp', 'tensor')
- attn_in_avg_new: float32 [6, 512, 512], P(None, 'dp', 'tensor')
- attn_out_grad: float32 [2, 512, 512], P(None, 'dp', 'tensor')
- attn_out_mom_new: float32 [2, 512, 512], P(None, 'dp', 'tensor')
- attn_out_new: float32 [2, 512, 512], P(None, 'dp', 'tensor')
- attn_out_avg_new: float32 [2, 512, 512], P(None, 'dp', 'tensor')
- ffn_in_grad: float32 [512, 2048], P('dp', 'tensor')
- ffn_in_mom_new: float32 [512, 2048], P('dp', 'tensor')
- ffn_in_new: float32 [512, 2048], P('dp', 'tensor')
- ffn_in_avg_new: float32 [512, 2048], P('dp', 'tensor')
- ffn_out_grad: float32 [512, 2048], P('dp', 'tensor')
- ffn_out_mom_new: float32 [512, 2048], P('dp', 'tensor')
- ffn_out_new: float32 [512, 2048], P('dp', 'tensor')
- ffn_out_avg_new: float32 [512, 2048], P('dp', 'tensor')
- norms_grad: float32 [6, 512], P(None, 'dp')
- norms_mom_new: float32 [6, 512], P(None, 'dp')
- norms_new: float32 [6, 512], P(None, 'dp')
- norms_avg_new: float32 [6, 512], P(None, 'dp')
The draws below stay inside these ranges and needn't reach their ends.
Inputs may be any that keep to these rules, and one draw needn't show every extreme that they name: Positions at and beyond a protein's length are padding; the largest length is 512 in every draw, and the lengths sum to 6144. The linker slots breaks to breaks + 9 are padding between the first and the second chain; where they lie at or beyond the length the complex holds one chain. `norms`: rows 0, 2, 4 are gains, rows 1, 3, 5 biases.
All inputs are finite; a program needn't handle non-finite values. No bound on the sum of `lengths` on one device may be relied on, other than what follows from the above.
Results may differ from the reference program's by a relative error of at most 0.02.
The reference program's roundings to bfloat16 on the way count: a program that leaves them out, or rounds other values in their place, can miss the bound.
Values may be sent and summed in bfloat16 or wider, within the bound.
A program may use at most 128 MiB of HBM per device.

```python
import math
import jax
import jax.numpy as jnp
import numpy as np
from jax import lax

D = 512
HEADS = 8
FF = 2048
HD = 64
SEQ = 512
LINKER = 10
PROTEINS = 16
TOKENS = 8192


def draw_norms(key, part):
    normal_draw = jnp.clip(jax.random.normal(key, (6, D), jnp.float32), -3.0, 3.0)
    row_index = lax.broadcasted_iota(jnp.int32, (6, D), 0)
    return jnp.where(row_index % 2 == 0, 1.0 + 0.1 * normal_draw, 0.3 * normal_draw)


def plant(result, key, least, largest):
    index_at = [jax.random.randint(jax.random.fold_in(key, axis), (), 0, length) for axis, length in enumerate(result.shape)]
    longest = result.shape.index(max(result.shape))
    beside = index_at[:longest] + [(index_at[longest] + 1) % result.shape[longest]] + index_at[longest + 1:]
    return result.at[tuple(index_at)].set(least).at[tuple(beside)].set(largest)


def shard_levels(key, shape, shards, low, largest):
    def one(axis_at, blocks):
        heights = jax.random.uniform(jax.random.fold_in(jax.random.fold_in(key, 6), axis_at), (blocks,), jnp.float32, low / len(shards), largest / len(shards))
        return jnp.repeat(jnp.exp(heights), shape[axis_at] // blocks).reshape((-1,) + (1,) * (len(shape) - axis_at - 1))

    loudness = one(*shards[0])
    for cut in shards[1:]:
        loudness = loudness * one(*cut)
    return loudness


def split_up(number_of, total, bound, lean):
    loads = [(1 << 20) // math.isqrt(standing ** lean) + 1 for standing in range(2, number_of + 1)]
    surplus, counts = total - bound - (number_of - 1), [1] * (number_of - 1)
    while surplus > 0:
        free = [i for i in range(number_of - 1) if counts[i] < bound]
        mass, remaining = sum([loads[i] for i in free]), surplus
        for i in free:
            extra = min(bound - counts[i], max(1, remaining * loads[i] // mass), surplus)
            counts[i] = counts[i] + extra
            surplus = surplus - extra
    return np.array([bound] + counts)


def ragged(key, number_of, total, limit, slope):
    if number_of == 2:
        one = jax.random.randint(key, (), max(1, total - limit), min(limit, total - 1) + 1)
        return jnp.stack([one, total - one])
    sizes = jnp.asarray(split_up(number_of, total, limit, slope), jnp.int32)
    pairs = (number_of - 1) // 2
    source_of, taker = sizes[1:1 + 2 * pairs:2], sizes[2:2 + 2 * pairs:2]
    room = jnp.minimum(source_of - 1, limit - taker)
    passed = jax.random.randint(jax.random.fold_in(key, 1), (pairs,), 0, 1 << 20) % (room + 1)
    sizes = sizes.at[1:1 + 2 * pairs:2].set(source_of - passed).at[2:2 + 2 * pairs:2].set(taker + passed)
    return sizes[jax.random.permutation(jax.random.fold_in(key, 2), number_of)]


def noise(rng, dims, scale, reach, pieces=(), dtype=jnp.bfloat16):
    level = shard_levels(rng, dims, pieces, -0.22, 0.18) if pieces else 1.0
    drawn = jax.random.normal(rng, dims, jnp.float32) * scale * level
    return jnp.minimum(jnp.maximum(drawn, -reach), reach).astype(dtype)


def setup_inputs(seed: int = 0) -> dict:
    splits = jax.random.split(jax.random.key(seed), 21)
    tokens = noise(splits[0], (TOKENS, D), 1.0, 6.0, ((0, 8),))
    memory = noise(splits[1], (TOKENS, D), 1.0, 6.0, ((0, 8),))
    cotangent = noise(splits[2], (TOKENS, D), 1.0, 6.0, ((0, 8),))
    lengths = ragged(splits[3], PROTEINS, 3 * TOKENS // 4, SEQ, 1).astype(jnp.int32)
    breaks = plant(jax.random.randint(splits[4], (PROTEINS,), 1, SEQ - LINKER), jax.random.fold_in(splits[4], 1), 1, (SEQ - LINKER) - 1).astype(jnp.int32)
    attn_in = noise(splits[5], (6, D, D), D ** -0.5, 0.25, ((1, 8), (2, 4)), jnp.float32)
    attn_out = noise(splits[6], (2, D, D), (max(1, 4 * D // SEQ)) ** -0.5, 3.0, ((1, 8), (2, 4)), jnp.float32)
    ffn_in = noise(splits[7], (D, FF), D ** -0.5, 0.25, ((0, 8), (1, 4)), jnp.float32)
    ffn_out = noise(splits[8], (D, FF), FF ** -0.5, 0.125, ((0, 8), (1, 4)), jnp.float32)
    norms = draw_norms(jax.random.fold_in(splits[20], 71), 0)
    attn_in_mom = noise(splits[10], (6, D, D), (TOKENS ** 0.5 / 2), 256.0, ((1, 8), (2, 4)), jnp.float32)
    attn_out_mom = noise(splits[11], (2, D, D), (TOKENS ** 0.5 / 8), 64.0, ((1, 8), (2, 4)), jnp.float32)
    ffn_in_mom = noise(splits[12], (D, FF), (TOKENS ** 0.5 / 2), 256.0, ((0, 8), (1, 4)), jnp.float32)
    ffn_out_mom = noise(splits[13], (D, FF), (TOKENS ** 0.5 / 2), 256.0, ((0, 8), (1, 4)), jnp.float32)
    norms_mom = noise(splits[14], (6, D), (TOKENS ** 0.5 / 2), 256.0, ((1, 8),), jnp.float32)
    attn_in_avg = noise(splits[15], (6, D, D), D ** -0.5, 0.25, ((1, 8), (2, 4)), jnp.float32)
    attn_out_avg = noise(splits[16], (2, D, D), (max(1, 4 * D // SEQ)) ** -0.5, 3.0, ((1, 8), (2, 4)), jnp.float32)
    ffn_in_avg = noise(splits[17], (D, FF), D ** -0.5, 0.25, ((0, 8), (1, 4)), jnp.float32)
    ffn_out_avg = noise(splits[18], (D, FF), FF ** -0.5, 0.125, ((0, 8), (1, 4)), jnp.float32)
    norms_avg = jnp.clip(1.0 + 0.1 * jax.random.normal(splits[19], (6, D), jnp.float32), 0.5, 1.5)
    return dict(tokens=tokens, memory=memory, cotangent=cotangent, lengths=lengths, breaks=breaks, attn_in=attn_in, attn_out=attn_out, ffn_in=ffn_in, ffn_out=ffn_out, norms=norms, attn_in_mom=attn_in_mom, attn_out_mom=attn_out_mom, ffn_in_mom=ffn_in_mom, ffn_out_mom=ffn_out_mom, norms_mom=norms_mom, attn_in_avg=attn_in_avg, attn_out_avg=attn_out_avg, ffn_in_avg=ffn_in_avg, ffn_out_avg=ffn_out_avg, norms_avg=norms_avg)


exact_mode = lax.Precision.HIGHEST
EPSILON = 1e-05
NEG_FILL = -1000000000.0
MOMENTUM = 0.9
AVG_DECAY = 0.6
BASE_RATES = (0.05, 1.0, 0.05, 0.05, 0.3)

@jax.custom_vjp
def low(v):
    return lax.optimization_barrier(v.astype(jnp.bfloat16)).astype(jnp.float32)

@jax.custom_vjp
def low_back(v):
    return v

def low_keep(v):
    return (low(v), None)

def low_pass(kept, grad):
    return (grad,)

def back_keep(v):
    return (v, None)

def back_low(kept, grad):
    return (low(grad),)
low.defvjp(low_keep, low_pass)
low_back.defvjp(back_keep, back_low)

def layer_norm(values, gain_row, bias_row):
    center = values - lax.optimization_barrier(jnp.mean(values, -1, keepdims=True))
    spread = lax.optimization_barrier(jnp.mean(center * center, -1, keepdims=True))
    return center * lax.rsqrt(spread + EPSILON) * gain_row + bias_row

def matmul_in(left_op, right_op):
    return jnp.dot(left_op, right_op, precision=exact_mode, preferred_element_type=jnp.float32)

def matmul_tr(left_op, right_op):
    return lax.dot_general(left_op, right_op, (((1,), (1,)), ((), ())), precision=exact_mode, preferred_element_type=jnp.float32)

def live_slots(length_n, break_n):
    positions = jnp.arange(SEQ)
    linker = (positions >= break_n) & (positions < break_n + LINKER)
    return (positions < length_n) & jnp.logical_not(linker)

def attend(query_src, key_src, w_query, w_key, w_value, mask_ok):
    seq_len = query_src.shape[0]
    query = low(low_back(matmul_in(query_src, w_query))).reshape(seq_len, HEADS, HD)
    keys_h = low(low_back(matmul_in(key_src, w_key))).reshape(seq_len, HEADS, HD)
    values_h = low(low_back(matmul_in(key_src, w_value))).reshape(seq_len, HEADS, HD)
    scores = jnp.einsum('qhe,khe->hqk', query, keys_h, precision=exact_mode) * HD ** (-0.5)
    scores = jnp.where(mask_ok[None], low_back(scores), NEG_FILL)
    top_score = lax.optimization_barrier(jnp.max(scores, -1, keepdims=True))
    expo = jnp.exp(scores - top_score)
    attn_prob = expo / lax.optimization_barrier(jnp.sum(expo, -1, keepdims=True))
    mixed = jnp.einsum('hqk,khe->qhe', low(attn_prob), values_h, precision=exact_mode)
    return low(low_back(mixed.reshape(seq_len, D)))

def layer(tokens_f, memory_f, length_n, break_n, params):
    w_in = low(params[0])
    w_out = low(params[1])
    w_up = low(params[2])
    w_down = low(params[3])
    norm_rows = low(params[4])
    positions = jnp.arange(SEQ)
    live = live_slots(length_n, break_n)
    key_live = live[None, :]
    self_ok = (positions[None, :] <= positions[:, None]) & key_live
    cross_ok = jnp.broadcast_to(key_live, (SEQ, SEQ))
    h_one = low(layer_norm(tokens_f, norm_rows[0], norm_rows[1]))
    x_one = tokens_f + low_back(matmul_tr(attend(h_one, h_one, w_in[0], w_in[1], w_in[2], self_ok), w_out[0]))
    h_two = low(layer_norm(x_one, norm_rows[2], norm_rows[3]))
    x_two = x_one + low_back(matmul_tr(attend(h_two, memory_f, w_in[3], w_in[4], w_in[5], cross_ok), w_out[1]))
    h_three = low(layer_norm(x_two, norm_rows[4], norm_rows[5]))
    hidden = low_back(matmul_in(h_three, w_up))
    act_low = low(jax.nn.gelu(hidden, approximate=False))
    return x_two + low_back(matmul_tr(act_low, w_down))

def update(weight, grad_sum, moment, average, rate):
    moment_new = MOMENTUM * moment + grad_sum
    weight_new = weight - rate * (grad_sum + MOMENTUM * moment_new)
    average_new = AVG_DECAY * average + (1.0 - AVG_DECAY) * weight_new
    return (moment_new, weight_new, average_new)

def reference(tokens, memory, cotangent, lengths, breaks, attn_in, attn_out, ffn_in, ffn_out, norms, attn_in_mom, attn_out_mom, ffn_in_mom, ffn_out_mom, norms_mom, attn_in_avg, attn_out_avg, ffn_in_avg, ffn_out_avg, norms_avg):
    params = (attn_in, attn_out, ffn_in, ffn_out, norms)
    tok_all = tokens.astype(jnp.float32).reshape(PROTEINS, SEQ, D)
    mem_all = memory.astype(jnp.float32).reshape(PROTEINS, SEQ, D)
    cot_all = cotangent.astype(jnp.float32).reshape(PROTEINS, SEQ, D)

    def one_protein(totals, item):
        tok_one, mem_one, cot_one, length_n, break_n = item

        def run(tok_arg, param_arg):
            return layer(tok_arg, mem_one, length_n, break_n, param_arg)
        out_one, pull = jax.vjp(run, tok_one, params)
        row_live = live_slots(length_n, break_n).astype(jnp.float32)[:, None]
        grad_tok, grad_params = pull(cot_one * row_live)
        return (jax.tree.map(jnp.add, totals, grad_params), (out_one.astype(jnp.bfloat16), grad_tok))
    zeros_init = jax.tree.map(jnp.zeros_like, params)
    grads, (outs, grad_toks) = lax.scan(one_protein, zeros_init, (tok_all, mem_all, cot_all, lengths, breaks))
    rate_scale = TOKENS ** (-0.5)
    in_m, in_w, in_a = update(attn_in, grads[0], attn_in_mom, attn_in_avg, BASE_RATES[0] * rate_scale)
    out_m, out_w, out_a = update(attn_out, grads[1], attn_out_mom, attn_out_avg, BASE_RATES[1] * rate_scale)
    up_m, up_w, up_a = update(ffn_in, grads[2], ffn_in_mom, ffn_in_avg, BASE_RATES[2] * rate_scale)
    down_m, down_w, down_a = update(ffn_out, grads[3], ffn_out_mom, ffn_out_avg, BASE_RATES[3] * rate_scale)
    norm_m, norm_w, norm_a = update(norms, grads[4], norms_mom, norms_avg, BASE_RATES[4] * rate_scale)
    return (outs.reshape(TOKENS, D), grad_toks.reshape(TOKENS, D), grads[0], in_m, in_w, in_a, grads[1], out_m, out_w, out_a, grads[2], up_m, up_w, up_a, grads[3], down_m, down_w, down_a, grads[4], norm_m, norm_w, norm_a)
```

```python
import functools

import jax
import jax.numpy as jnp
from jax import lax
from jax.experimental import pallas as pl
from jax.experimental.pallas import tpu as pltpu
from jax.sharding import PartitionSpec as P

HD = 64
SEQ = 512
WIDTH = 512
LINKER = 10
EPSILON = 1e-05
NEG_FILL = -1000000000.0
MOMENTUM = 0.9
AVG_DECAY = 0.6
BASE_RATES = (0.05, 1.0, 0.05, 0.05, 0.3)

BF = jnp.bfloat16
F32 = jnp.float32
MESH = pl.DeviceIdType.MESH
HEADS_HERE = 4
COLS = 256
BLOCKS = 16
GROUPS = 8
BLOCK_OF = (
    (0, 0), (0, 1), (0, 2), (1, 0),
    (0, 4), (0, 5), (0, 3), (1, 1),
    (2, 0), (3, 0), (2, 1), (3, 1),
    (2, 2), (3, 2), (2, 3), (3, 3),
)
WQ1, WK1, WV1, WO1, WK2, WV2, WQ2, WO2 = range(8)


def nn(left, right):
    return jnp.dot(left, right, preferred_element_type=F32)


def nt(left, right):
    return lax.dot_general(left, right, (((1,), (1,)), ((), ())), preferred_element_type=F32)


def layer_kernel(
    nz,
    tok_hbm, mem_hbm, cot_hbm, len_ref, brk_ref, ain, aout, fin, fout, norms,
    gsum, nsum, bout, tgrad,
    tok, mem, cot, W, G, R1A, R1B, R2, RZ, NB, NP, GAIN, NGR, NX, NY, NZB, NT,
    XS, XR, XF, XH, IV, OACC, DHA, H, HT, Q, K, V, KM, VM, PR, DS, A, DX, DQ, DK, DV,
    ACT, DU, DZ, DO, TR,
    lsem, ag_zs, ag_zr, ag_ms, ag_mr, nb_s, nb_r, xc_s, xc_r, rs_ms, rs_mr, rs_zs, rs_zr,
    ng_s, ng_r, out_s, out_r,
):
    dp, tensor = lax.axis_index("dp"), lax.axis_index("tensor")
    z, y, x, core = dp // 2, dp % 2, tensor // 2, tensor % 2
    rows_own = ain.shape[1]
    sibling = (dp, x * 2 + 1 - core)
    x_peer = (dp, (1 - x) * 2 + core)
    y_peer = (z * 2 + 1 - y, tensor)
    z_of = [None] + [lax.rem(z + step, nz) for step in range(1, nz)]
    z_peer = [None] + [(z_of[step] * 2 + y, tensor) for step in range(1, nz)]
    pending = []

    def send(src, dst, send_sem, recv_sem, peer):
        copy = pltpu.make_async_remote_copy(
            src, dst, send_sem, recv_sem, device_id=peer, device_id_type=MESH
        )
        copy.start()
        pending.append(copy)
        return copy

    barrier = pltpu.get_barrier_semaphore()
    peers = [sibling, x_peer, y_peer] + z_peer[1:]
    for peer in peers:
        pl.semaphore_signal(barrier, inc=1, device_id=peer, device_id_type=MESH)
    fetches = []
    for number, (src, dst) in enumerate(((tok_hbm, tok), (mem_hbm, mem), (cot_hbm, cot))):
        fetch = pltpu.make_async_copy(
            src.at[pl.ds(pl.multiple_of(x * SEQ, SEQ), SEQ)], dst, lsem.at[number]
        )
        fetch.start()
        fetches.append(fetch)

    NP[...] = jnp.zeros_like(NP)
    NP[0:6, 0:rows_own] = norms[...].astype(BF).astype(F32)
    lane_at = lax.rem(dp * rows_own, 128)
    NB[z, y] = pltpu.roll(NP[...], lane_at, 1)

    def own_block(arrays, block):
        array, index = BLOCK_OF[block]
        if array < 2:
            return arrays[array][index]
        return arrays[array][:, index * 128 : (index + 1) * 128]

    for block in range(BLOCKS):
        W[x, block, z, y] = own_block((ain, aout, fin, fout), block).astype(BF)
    pl.semaphore_wait(barrier, len(peers))

    ag_first, ag_second, ag_third, nb_first = {}, {}, {}, []

    def blocks_of(group):
        return pl.ds(2 * group, 2)

    def gather_start(group):
        part = W.at[x, blocks_of(group), z, y]
        ag_first[group] = [
            send(part, part, ag_zs.at[group, s - 1], ag_zr.at[group, s - 1], z_peer[s])
            for s in range(1, nz)
        ]

    def gather_mid(group):
        for copy in ag_first[group]:
            copy.wait_recv()
        part = W.at[x, blocks_of(group), :, y]
        peer = y_peer if group % 2 == 0 else x_peer
        ag_second[group] = send(part, part, ag_ms.at[0, group], ag_mr.at[0, group], peer)

    def gather_last(group):
        ag_second[group].wait_recv()
        if group % 2 == 0:
            part, peer = W.at[x, blocks_of(group)], x_peer
        else:
            part, peer = W.at[:, blocks_of(group), :, y], y_peer
        ag_third[group] = send(part, part, ag_ms.at[1, group], ag_mr.at[1, group], peer)

    def gather_done(group):
        ag_third[group].wait_recv()

    nb_first = [
        send(NB.at[z, y], NB.at[z, y], nb_s.at[s - 1], nb_r.at[s - 1], z_peer[s])
        for s in range(1, nz)
    ]
    for group in range(GROUPS):
        gather_start(group)

    def weight(block):
        return jnp.concatenate(
            [W[0, block].reshape(WIDTH, 128), W[1, block].reshape(WIDTH, 128)], axis=1
        )

    rs_first, rs_second, rs_third = {}, {}, {}

    def put_grad(block, value):
        low = value.astype(BF)
        G[0, block] = low[:, :128].reshape(G.shape[2:])
        G[1, block] = low[:, 128:].reshape(G.shape[2:])

    def sum_start(group):
        slot = pl.ds(2 * (group // 2), 2)
        if group % 2 == 0:
            src, dst, peer = G.at[1 - x, blocks_of(group)], R1A.at[slot], x_peer
        else:
            src, dst, peer = G.at[:, blocks_of(group), :, 1 - y], R1B.at[:, slot], y_peer
        rs_first[group] = send(src, dst, rs_ms.at[0, group], rs_mr.at[0, group], peer)

    def sum_mid(group):
        rs_first[group].wait_recv()
        for number in range(2):
            block, slot = 2 * group + number, 2 * (group // 2) + number
            if group % 2 == 0:
                G[x, block] = (G[x, block].astype(F32) + R1A[slot].astype(F32)).astype(BF)
            else:
                for side in range(2):
                    G[side, block, :, y] = (
                        G[side, block, :, y].astype(F32) + R1B[side, slot].astype(F32)
                    ).astype(BF)
        if group % 2 == 0:
            src, peer = G.at[x, blocks_of(group), :, 1 - y], y_peer
        else:
            src, peer = G.at[1 - x, blocks_of(group), :, y], x_peer
        rs_second[group] = send(
            src, R2.at[blocks_of(group)], rs_ms.at[1, group], rs_mr.at[1, group], peer
        )

    def sum_last(group):
        rs_second[group].wait_recv()
        for number in range(2):
            block = 2 * group + number
            G[x, block, :, y] = (
                G[x, block, :, y].astype(F32) + R2[block].astype(F32)
            ).astype(BF)
        rs_third[group] = [
            send(
                G.at[x, blocks_of(group), z_of[s], y],
                RZ.at[s - 1, blocks_of(group)],
                rs_zs.at[group, s - 1],
                rs_zr.at[group, s - 1],
                z_peer[s],
            )
            for s in range(1, nz)
        ]

    def sum_done(group):
        for copy in rs_third[group]:
            copy.wait_recv()
        for number in range(2):
            block = 2 * group + number
            total = G[x, block, z, y].astype(F32)
            for s in range(1, nz):
                total = total + RZ[s - 1, block].astype(F32)
            gsum[block] = total

    xc = {}

    def swap_start(number, half):
        rows = pl.ds(half * 256, 256)
        xc[number, half] = send(
            XS.at[number, rows],
            XR.at[number, rows],
            xc_s.at[number, half],
            xc_r.at[number, half],
            sibling,
        )

    def swap_sum(number, rows):
        return XS[number, rows].astype(F32) + XR[number, rows].astype(F32)

    def swap_rows(number, make):
        for half in range(2):
            rows = slice(half * 256, half * 256 + 256)
            XS[number, rows] = make(rows).astype(BF)
            swap_start(number, half)

    def each_rows(body, size=128, start=0, stop=SEQ):
        def one(step, carry):
            body(pl.ds(pl.multiple_of(start + step * size, size), size), start + step * size)
            return carry

        lax.fori_loop(0, (stop - start) // size, one, 0)

    def norm_rows(number, rows, values):
        center = values - jnp.mean(values, -1, keepdims=True)
        inv_std = lax.rsqrt(jnp.mean(center * center, -1, keepdims=True) + EPSILON)
        x_hat = center * inv_std
        XH[number, rows] = x_hat
        IV[number, rows] = inv_std
        gain, bias = GAIN[2 * number : 2 * number + 1], GAIN[2 * number + 1 : 2 * number + 2]
        H[number, rows] = (x_hat * gain + bias).astype(BF)

    def norm_back(number, rows, grad_h):
        x_hat, inv_std = XH[number, rows], IV[number, rows]
        NGR[2 * number] += jnp.sum((grad_h * x_hat).reshape(-1, 8, WIDTH), 0)
        NGR[2 * number + 1] += jnp.sum(grad_h.reshape(-1, 8, WIDTH), 0)
        grad_hat = grad_h * GAIN[2 * number : 2 * number + 1]
        return inv_std * (
            grad_hat
            - jnp.mean(grad_hat, -1, keepdims=True)
            - x_hat * jnp.mean(grad_hat * x_hat, -1, keepdims=True)
        )

    length_n, break_n = len_ref[x], brk_ref[x]

    def live_of(places):
        linker = (places >= break_n) & (places < break_n + LINKER)
        return (places < length_n) & jnp.logical_not(linker)

    def key_fill(count):
        places = lax.broadcasted_iota(jnp.int32, (1, count), 1)
        return jnp.where(live_of(places), 0.0, NEG_FILL)

    head_of = lax.broadcasted_iota(jnp.int32, (1, COLS), 1) // HD

    def split_heads(number):
        keys, values = K[number], V[number]
        for head in range(HEADS_HERE):
            KM[number, head] = jnp.where(head_of == head, keys, jnp.zeros_like(keys))
            VM[number, head] = jnp.where(head_of == head, values, jnp.zeros_like(values))

    def attend(number, half):
        count = 256 * (half + 1) if number == 0 else SEQ
        fill = key_fill(count)

        def body(rows, first):
            bias = fill
            if number == 0:
                row = first + lax.broadcasted_iota(jnp.int32, (128, count), 0)
                col = lax.broadcasted_iota(jnp.int32, (128, count), 1)
                bias = jnp.where(col <= row, fill, NEG_FILL)
            query = Q[number, rows]
            mixed = jnp.zeros((128, COLS), F32)
            for head in range(HEADS_HERE):
                scores = nt(query, KM[number, head, :count]) + bias
                expo = jnp.exp(scores - jnp.max(scores, -1, keepdims=True))
                prob = (expo * (1.0 / jnp.sum(expo, -1, keepdims=True))).astype(BF)
                PR[number, head, rows, :count] = prob
                mixed = mixed + nn(prob, VM[number, head, :count])
            A[number, rows] = mixed.astype(BF)

        each_rows(body, start=half * 256, stop=half * 256 + 256)

    def attend_back(number, half):
        count = 256 * (half + 1) if number == 0 else SEQ

        def body(rows, first):
            grad_o = DO[rows]
            grad_q = jnp.zeros((128, COLS), F32)
            for head in range(HEADS_HERE):
                grad_p = nt(grad_o, VM[number, head, :count])
                prob = PR[number, head, rows, :count].astype(F32)
                inner = jnp.sum(prob * grad_p, -1, keepdims=True)
                grad_s = (prob * (grad_p - inner)).astype(BF)
                DS[head, rows, :count] = grad_s
                grad_q = grad_q + nn(grad_s, KM[number, head, :count])
            DQ[rows] = (grad_q * HD**-0.5).astype(BF)

        each_rows(body, start=half * 256, stop=half * 256 + 256)

    def attend_keys(number):
        for table, source, target in ((PR.at[number], DO, DV), (DS, Q.at[number], DK)):
            source_t = source[...].T
            for head in range(HEADS_HERE):
                part = slice(head * HD, (head + 1) * HD)
                if number == 0:
                    TR[part, 0:256] = nn(source_t[part], table[head, :, 0:256]).astype(BF)
                    TR[part, 256:512] = nn(
                        source_t[part, 256:512], table[head, 256:512, 256:512]
                    ).astype(BF)
                else:
                    TR[part] = nn(source_t[part], table[head]).astype(BF)
            target[...] = TR[...].T

    for copy in nb_first:
        copy.wait_recv()
    nb_second = send(NB.at[:, y], NB.at[:, y], nb_s.at[nz - 1], nb_r.at[nz - 1], y_peer)
    gather_mid(0)
    gather_mid(1)
    nb_second.wait_recv()
    per_column = nz // 4
    for column in range(4):
        total = NB[column * per_column, 0] + NB[column * per_column, 1]
        for extra in range(1, per_column):
            total = total + NB[column * per_column + extra, 0] + NB[column * per_column + extra, 1]
        GAIN[:, column * 128 : (column + 1) * 128] = total
    NGR[...] = jnp.zeros_like(NGR)
    for fetch in fetches:
        fetch.wait()
    each_rows(lambda rows, first: norm_rows(0, rows, tok[rows].astype(F32)))
    HT[0] = H[0].T
    HT[1] = mem[...].T

    def dead_rows(rows, first):
        places = first + lax.broadcasted_iota(jnp.int32, (128, 1), 0)
        DZ[rows] = jnp.where(live_of(places), cot[rows].astype(F32), 0.0).astype(BF)

    each_rows(dead_rows)
    HT[4] = DZ[...].T
    gather_last(0)
    gather_last(1)
    gather_mid(2)
    gather_mid(3)
    gather_done(0)
    Q[0] = (nn(H[0], weight(WQ1)) * HD**-0.5).astype(BF)
    K[0] = nn(H[0], weight(WK1)).astype(BF)
    gather_done(1)
    V[0] = nn(H[0], weight(WV1)).astype(BF)
    gather_last(2)
    gather_last(3)
    split_heads(0)
    attend(0, 0)
    gather_mid(4)
    gather_mid(5)
    attend(0, 1)
    out_w = weight(WO1)
    swap_rows(0, lambda rows: nt(A[0, rows], out_w))
    gather_done(2)
    K[1] = nn(mem[...], weight(WK2)).astype(BF)
    V[1] = nn(mem[...], weight(WV2)).astype(BF)
    split_heads(1)
    gather_last(4)
    gather_last(5)

    def second_rows(rows, first):
        values = tok[rows].astype(F32) + swap_sum(0, rows)
        XF[rows] = values
        norm_rows(1, rows, values)

    xc[0, 0].wait_recv()
    xc[0, 1].wait_recv()
    each_rows(second_rows)
    gather_mid(6)
    gather_mid(7)
    gather_done(3)
    Q[1] = (nn(H[1], weight(WQ2)) * HD**-0.5).astype(BF)
    attend(1, 0)
    attend(1, 1)
    out_w = weight(WO2)
    swap_rows(1, lambda rows: nt(A[1, rows], out_w))
    gather_last(6)
    gather_last(7)
    HT[2] = H[1].T

    def third_rows(rows, first):
        values = XF[rows] + swap_sum(1, rows)
        XF[rows] = values
        norm_rows(2, rows, values)

    xc[1, 0].wait_recv()
    xc[1, 1].wait_recv()
    each_rows(third_rows)
    HT[3] = H[2].T

    for chunk in range(4):
        gather_done(4 + chunk)
        up, down = weight(8 + 2 * chunk), weight(9 + 2 * chunk)

        def hidden_rows(rows, first):
            hidden = nn(H[2, rows], up)
            grad_act = nn(DZ[rows], down)
            gate = 0.5 + 0.5 * lax.erf(hidden * 0.5**0.5)
            slope = gate + hidden * jnp.exp(-0.5 * hidden * hidden) * 0.3989422804014327
            act = (hidden * gate).astype(BF)
            grad_u = (grad_act * slope).astype(BF)
            ACT[rows] = act
            DU[rows] = grad_u
            if chunk == 0:
                OACC[rows] = nt(act, down)
                DHA[rows] = nt(grad_u, up)
            else:
                OACC[rows] += nt(act, down)
                DHA[rows] += nt(grad_u, up)

        each_rows(hidden_rows, size=256)
        put_grad(8 + 2 * chunk, nn(HT[3], DU[...]))
        put_grad(9 + 2 * chunk, nn(HT[4], ACT[...]))
        sum_start(4 + chunk)

    swap_rows(3, lambda rows: DHA[rows])
    swap_rows(2, lambda rows: OACC[rows])
    sum_mid(4)
    sum_mid(5)

    def back_third(rows, first):
        grad_out = DZ[rows].astype(F32)
        grad = grad_out + norm_back(2, rows, swap_sum(3, rows))
        DX[rows] = grad
        H[2, rows] = grad.astype(BF)

    xc[3, 0].wait_recv()
    xc[3, 1].wait_recv()
    each_rows(back_third)
    DO[...] = nn(H[2], weight(WO2)).astype(BF)
    put_grad(WO2, nn(H[2].T, A[1]))
    sum_mid(6)
    sum_mid(7)
    attend_back(1, 0)
    attend_back(1, 1)
    up = weight(WQ2)
    swap_rows(4, lambda rows: nt(DQ[rows], up))
    put_grad(WQ2, nn(HT[2], DQ[...]))
    sum_start(3)
    sum_last(4)
    sum_last(5)
    attend_keys(1)
    put_grad(WK2, nn(HT[1], DK[...]))
    put_grad(WV2, nn(HT[1], DV[...]))
    sum_start(2)

    def out_rows(rows, first):
        bout[x, rows] = (XF[rows] + swap_sum(2, rows)).astype(BF)

    half_own = pl.ds(pl.multiple_of(core * 256, 256), 256)

    def share_start(number, result):
        part = result.at[x, half_own]
        return send(part, part, out_s.at[number, 0], out_r.at[number, 0], x_peer)

    def share_pass(number, result):
        part = result.at[1 - x, half_own]
        return send(part, part, out_s.at[number, 1], out_r.at[number, 1], sibling)

    xc[2, 0].wait_recv()
    xc[2, 1].wait_recv()
    each_rows(out_rows)
    share_out = share_start(0, bout)

    def back_second(rows, first):
        grad = DX[rows] + norm_back(1, rows, swap_sum(4, rows))
        DX[rows] = grad
        H[2, rows] = grad.astype(BF)

    xc[4, 0].wait_recv()
    xc[4, 1].wait_recv()
    each_rows(back_second)
    DO[...] = nn(H[2], weight(WO1)).astype(BF)
    put_grad(WO1, nn(H[2].T, A[0]))
    sum_last(6)
    sum_last(7)
    attend_back(0, 0)
    sum_mid(3)
    attend_back(0, 1)
    sum_mid(2)
    attend_keys(0)
    put_grad(WV1, nn(HT[0], DV[...]))
    sum_start(1)
    put_grad(WQ1, nn(HT[0], DQ[...]))
    put_grad(WK1, nn(HT[0], DK[...]))
    sum_start(0)
    w_q, w_k, w_v = weight(WQ1), weight(WK1), weight(WV1)
    swap_rows(5, lambda rows: nt(DQ[rows], w_q) + nt(DK[rows], w_k) + nt(DV[rows], w_v))
    share_out.wait_recv()
    share_out2 = share_pass(0, bout)
    sum_last(3)
    sum_last(2)
    for group in (4, 5, 6, 7):
        sum_done(group)

    def back_first(rows, first):
        grad = DX[rows] + norm_back(0, rows, swap_sum(5, rows))
        tgrad[x, rows] = grad.astype(BF)

    xc[5, 0].wait_recv()
    xc[5, 1].wait_recv()
    each_rows(back_first)
    share_grad = share_start(1, tgrad)

    for row in range(6):
        NX[0, row : row + 1] = jnp.sum(NGR[row], 0, keepdims=True)
    NX[0, 6:8] = jnp.zeros((2, WIDTH), F32)
    norm_x = send(NX.at[0], NX.at[1], ng_s.at[0], ng_r.at[0], x_peer)
    sum_mid(1)
    norm_x.wait_recv()
    NY[0] = NX[0] + NX[1]
    norm_y = send(NY.at[0], NY.at[1], ng_s.at[1], ng_r.at[1], y_peer)
    sum_mid(0)
    sum_done(3)
    norm_y.wait_recv()
    NZB[nz - 1] = NY[0] + NY[1]
    norm_z = [
        send(NZB.at[nz - 1], NZB.at[s - 1], ng_s.at[1 + s], ng_r.at[1 + s], z_peer[s])
        for s in range(1, nz)
    ]
    sum_done(2)
    sum_last(1)
    sum_last(0)
    share_grad.wait_recv()
    share_grad2 = share_pass(1, tgrad)
    total = NZB[nz - 1]
    for s in range(1, nz):
        norm_z[s - 1].wait_recv()
        total = total + NZB[s - 1]
    NT[...] = total
    column = pl.ds(pl.multiple_of(dp * rows_own // 128 * 128, 128), 128)
    nsum[...] = pltpu.roll(NT[:, column], lax.rem(128 - lane_at, 128), 1)
    sum_done(1)
    sum_done(0)
    share_out2.wait_recv()
    share_grad2.wait_recv()
    for copy in pending:
        copy.wait_send()


def update(weight, grad, moment, average, rate):
    moment_new = MOMENTUM * moment + grad
    weight_new = weight - rate * (grad + MOMENTUM * moment_new)
    average_new = AVG_DECAY * average + (1.0 - AVG_DECAY) * weight_new
    return moment_new, weight_new, average_new


def update_kernel(rate_scale, gsum, nsum, tlow, *refs):
    weights, moments, averages, outs = refs[0:5], refs[5:10], refs[10:15], refs[15:]
    tgrad_out, results = outs[0], outs[1:]
    tgrad_out[...] = tlow[...].astype(F32)

    def one(which, at, grad):
        found = update(
            weights[which][at],
            grad,
            moments[which][at],
            averages[which][at],
            BASE_RATES[which] * rate_scale,
        )
        for number, value in enumerate((grad, *found)):
            results[4 * which + number][at] = value

    for block, (array, index) in enumerate(BLOCK_OF):
        at = (index,) if array < 2 else (slice(None), slice(index * 128, index * 128 + 128))
        one(array, at, gsum[block])
    wide = weights[4].shape[1]
    one(4, (slice(None), slice(None)), nsum[0:6, 0:wide])


def per_device(nz, *args):
    (tokens, memory, cotangent, lengths, breaks, attn_in, attn_out, ffn_in, ffn_out, norms) = args[:10]
    moments, averages = args[10:15], args[15:20]
    own = attn_in.shape[1]
    whole = (nz, 2, own, 128)
    vmem = pl.BlockSpec(memory_space=pltpu.VMEM)
    smem = pl.BlockSpec(memory_space=pltpu.SMEM)
    hbm = pl.BlockSpec(memory_space=pl.ANY)
    dma = pltpu.SemaphoreType.DMA

    def bf(*shape):
        return pltpu.VMEM(shape, BF)

    def f32(*shape):
        return pltpu.VMEM(shape, F32)

    scratch = [
        bf(SEQ, WIDTH), bf(SEQ, WIDTH), bf(SEQ, WIDTH),
        bf(2, BLOCKS, *whole), bf(2, BLOCKS, *whole),
        bf(8, *whole), bf(2, 8, nz, own, 128), bf(BLOCKS, nz, own, 128),
        bf(nz - 1, BLOCKS, own, 128),
        f32(nz, 2, 8, 128), f32(8, 128), f32(8, WIDTH),
        f32(6, 8, WIDTH), f32(2, 8, WIDTH), f32(2, 8, WIDTH), f32(nz, 8, WIDTH),
        f32(8, WIDTH),
        bf(6, SEQ, WIDTH), bf(6, SEQ, WIDTH),
        f32(SEQ, WIDTH), f32(3, SEQ, WIDTH), f32(3, SEQ, 1),
        f32(SEQ, WIDTH), f32(SEQ, WIDTH),
        bf(3, SEQ, WIDTH), bf(5, WIDTH, SEQ),
        bf(2, SEQ, COLS), bf(2, SEQ, COLS), bf(2, SEQ, COLS),
        bf(2, HEADS_HERE, SEQ, COLS), bf(2, HEADS_HERE, SEQ, COLS),
        bf(2, HEADS_HERE, SEQ, SEQ), bf(HEADS_HERE, SEQ, SEQ),
        bf(2, SEQ, COLS), f32(SEQ, WIDTH),
        bf(SEQ, COLS), bf(SEQ, COLS), bf(SEQ, COLS),
        bf(SEQ, COLS), bf(SEQ, COLS), bf(SEQ, WIDTH), bf(SEQ, COLS), bf(COLS, SEQ),
        dma((3,)), dma((GROUPS, nz - 1)), dma((GROUPS, nz - 1)),
        dma((2, GROUPS)), dma((2, GROUPS)), dma((nz,)), dma((nz,)),
        dma((6, 2)), dma((6, 2)),
        dma((2, GROUPS)), dma((2, GROUPS)), dma((GROUPS, nz - 1)), dma((GROUPS, nz - 1)),
        dma((nz + 1,)), dma((nz + 1,)), dma((2, 2)), dma((2, 2)),
    ]
    gsum, nsum, bout, tlow = pl.pallas_call(
        functools.partial(layer_kernel, nz),
        out_shape=(
            jax.ShapeDtypeStruct((BLOCKS, own, 128), F32),
            jax.ShapeDtypeStruct((8, 128), F32),
            jax.ShapeDtypeStruct((2, SEQ, WIDTH), BF),
            jax.ShapeDtypeStruct((2, SEQ, WIDTH), BF),
        ),
        in_specs=[hbm] * 3 + [smem] * 2 + [vmem] * 5,
        out_specs=(vmem,) * 4,
        scratch_shapes=scratch,
        compiler_params=pltpu.CompilerParams(
            collective_id=0, has_side_effects=True, vmem_limit_bytes=58 * 2**20
        ),
    )(tokens, memory, cotangent, lengths, breaks, attn_in, attn_out, ffn_in, ffn_out, norms)
    weights = (attn_in, attn_out, ffn_in, ffn_out, norms)
    rate_scale = float(lax.axis_size("dp") * tokens.shape[0]) ** -0.5
    results = pl.pallas_call(
        functools.partial(update_kernel, rate_scale),
        out_shape=(jax.ShapeDtypeStruct((2, SEQ, WIDTH), F32),)
        + tuple(jax.ShapeDtypeStruct(w.shape, F32) for w in weights for _ in range(4)),
        compiler_params=pltpu.CompilerParams(vmem_limit_bytes=32 * 2**20),
    )(gsum, nsum, tlow, *weights, *moments, *averages)
    return (bout.reshape(tokens.shape), results[0].reshape(tokens.shape), *results[1:])


def solution(mesh):
    rows, attn, ffn, norm = P("dp", None), P(None, "dp", "tensor"), P("dp", "tensor"), P(None, "dp")
    weights = (attn, attn, ffn, ffn, norm)
    return jax.shard_map(
        functools.partial(per_device, mesh.shape["dp"] // 2),
        mesh=mesh,
        in_specs=(rows, rows, rows, P("dp"), P("dp")) + weights * 3,
        out_specs=(rows, rows) + tuple(spec for spec in weights for _ in range(4)),
        check_vma=False,
    )
```

```python
import functools

import jax
import jax.numpy as jnp
from jax import lax
from jax.experimental import pallas as pl
from jax.experimental.pallas import tpu as pltpu
from jax.sharding import PartitionSpec as P

HD = 64
SEQ = 512
WIDTH = 512
LINKER = 10
EPSILON = 1e-05
NEG_FILL = -1000000000.0
MOMENTUM = 0.9
AVG_DECAY = 0.6
BASE_RATES = (0.05, 1.0, 0.05, 0.05, 0.3)

BF = jnp.bfloat16
F32 = jnp.float32
MESH = pl.DeviceIdType.MESH
HEADS_HERE = 4
COLS = 256
BLOCKS = 16
BLOCK_OF = (
    (0, 0), (0, 1), (0, 2), (1, 0),
    (0, 4), (0, 5), (0, 3), (1, 1),
    (2, 0), (3, 0), (2, 1), (3, 1),
    (2, 2), (3, 2), (2, 3), (3, 3),
)
WQ1, WK1, WV1, WO1, WK2, WV2, WQ2, WO2 = range(8)
GATHER = tuple((block, 1, ("zyx", "zxy")[block % 2]) for block in range(14)) + ((14, 1, "xyz"), (15, 1, "yxz"))
SUM = (
    (8, 1, "zyx"), (9, 1, "zxy"), (10, 1, "xyz"), (11, 1, "yxz"),
    (12, 1, "xyz"), (13, 1, "yxz"), (14, 1, "yzx"), (15, 1, "yxz"),
    (7, 1, "yzx"), (5, 1, "xyz"), (6, 1, "yxz"), (4, 1, "yxz"),
    (3, 1, "yzx"), (2, 1, "yxz"), (0, 1, "xyz"), (1, 1, "yxz"),
)


def nn(left, right):
    return jnp.dot(left, right, preferred_element_type=F32)


def nt(left, right):
    return lax.dot_general(left, right, (((1,), (1,)), ((), ())), preferred_element_type=F32)


def layer_kernel(
    nz,
    tok_hbm, mem_hbm, cot_hbm, len_ref, brk_ref, ain, aout, fin, fout, norms,
    gsum, nsum, bout, tgrad,
    tok, mem, cot, W, G, R, NB, NP, GAIN, NGR, NX, NY, NZB, NT,
    XS, XR, XF, XH, IV, OACC, DHA, H, HT, Q, K, V, KM, VM, PR, DS, A, DX, DQ, DK, DV,
    ACT, DU, DZ, DO, TR,
    lsem, ag_s, ag_r, rs_s, rs_r, nb_s, nb_r, xc_s, xc_r,
    ng_s, ng_r, out_s, out_r,
):
    dp, tensor = lax.axis_index("dp"), lax.axis_index("tensor")
    z, y, x, core = dp // 2, dp % 2, tensor // 2, tensor % 2
    rows_own = ain.shape[1]
    sibling = (dp, x * 2 + 1 - core)
    x_peer = (dp, (1 - x) * 2 + core)
    y_peer = (z * 2 + 1 - y, tensor)
    z_of = [None] + [lax.rem(z + step, nz) for step in range(1, nz)]
    z_peer = [None] + [(z_of[step] * 2 + y, tensor) for step in range(1, nz)]
    pending = []

    def send(src, dst, send_sem, recv_sem, peer, alone=True):
        copy = pltpu.make_async_remote_copy(
            src, dst, send_sem, recv_sem, device_id=peer, device_id_type=MESH
        )
        copy.start()
        if alone:
            pending.append(copy)
        return copy

    barrier = pltpu.get_barrier_semaphore()
    peers = [sibling, x_peer, y_peer] + z_peer[1:]
    for peer in peers:
        pl.semaphore_signal(barrier, inc=1, device_id=peer, device_id_type=MESH)
    fetches = []
    for number, (src, dst) in enumerate(((tok_hbm, tok), (mem_hbm, mem), (cot_hbm, cot))):
        fetch = pltpu.make_async_copy(
            src.at[pl.ds(pl.multiple_of(x * SEQ, SEQ), SEQ)], dst, lsem.at[number]
        )
        fetch.start()
        fetches.append(fetch)

    NP[...] = jnp.zeros_like(NP)
    NP[0:6, 0:rows_own] = norms[...].astype(BF).astype(F32)
    lane_at = lax.rem(dp * rows_own, 128)
    NB[z, y] = pltpu.roll(NP[...], lane_at, 1)

    def own_block(arrays, block):
        array, index = BLOCK_OF[block]
        if array < 2:
            return arrays[array][index]
        return arrays[array][:, index * 128 : (index + 1) * 128]

    for block in range(BLOCKS):
        W[x, block, z, y] = own_block((ain, aout, fin, fout), block).astype(BF)
    pl.semaphore_wait(barrier, len(peers))

    me_of = {"x": x, "y": y, "z": z}
    flights, nb_second = {}, []

    def send_all(key, axis, pieces, whole, sems):
        if axis == "z":
            copies = [(z_of[s], s - 1, z_peer[s]) for s in range(1, nz)]
        elif axis == "y":
            copies = [(1 - y, 0, y_peer)]
        else:
            copies = [(1 - x, 0, x_peer)]
        for place, slot, peer in copies:
            send(*pieces(place, slot), *sems, peer, False)
        flights[key] = pltpu.make_async_remote_copy(
            *whole, *sems, device_id=copies[0][2], device_id_type=MESH
        )
        pending.append(flights[key])

    def landed(key):
        flights[key].wait_recv()

    def place_of(done, blocks):
        at = {axis: slice(None) if axis in done else me_of[axis] for axis in "xyz"}
        return at, lambda: (at["x"], blocks, at["z"], at["y"])

    def gather(parcel, phase):
        if phase > 0:
            landed(("gather", parcel, phase - 1))
        if phase == 3:
            return
        first, count, route = GATHER[parcel]
        at, where = place_of(route[:phase], pl.ds(first, count))
        part = W.at[where()]
        sems = (ag_s.at[parcel, phase], ag_r.at[parcel, phase])
        if route[phase] == "z":
            at["z"] = pl.ds(0, nz - 1)
        much = W.at[where()]
        send_all(
            ("gather", parcel, phase), route[phase], lambda place, slot: (part, part), (much, much), sems
        )

    nb_first = [
        send(NB.at[z, y], NB.at[z, y], nb_s.at[s - 1], nb_r.at[s - 1], z_peer[s])
        for s in range(1, nz)
    ]

    def weight(block):
        return jnp.concatenate(
            [W[0, block].reshape(WIDTH, 128), W[1, block].reshape(WIDTH, 128)], axis=1
        )

    def put_grad(block, value):
        low = value.astype(BF)
        G[0, block] = low[:, :128].reshape(G.shape[2:])
        G[1, block] = low[:, 128:].reshape(G.shape[2:])

    def total(parcel, phase):
        first, count, route = SUM[parcel]
        if phase > 0:
            landed(("sum", parcel, phase - 1))
            into = R[parcel][phase - 1]
            left = [axis for axis in "xyz" if axis not in route[:phase]]
            at, _ = place_of([axis for axis in left], None)
            for number in range(count):
                for side in range(2) if "x" in left else (x,):
                    here = (side, first + number, at["z"], at["y"])
                    found = G[here].astype(F32)
                    for slot in range(nz - 1 if route[phase - 1] == "z" else 1):
                        landing = into[slot, side, number] if "x" in left else into[slot, number]
                        found = found + landing.astype(F32)
                    if phase == 3:
                        gsum[first + number] = found
                    else:
                        G[here] = found.astype(BF)
        if phase == 3:
            return
        axis, into = route[phase], R[parcel][phase]
        at, where = place_of([a for a in "xyz" if a not in route[:phase]], pl.ds(first, count))

        def pieces(place, slot):
            at[axis] = place
            return G.at[where()], into.at[slot]

        at[axis] = pl.ds(0, nz - 1) if axis == "z" else me_of[axis]
        much = G.at[where()]
        sems = (rs_s.at[parcel, phase], rs_r.at[parcel, phase])
        send_all(("sum", parcel, phase), axis, pieces, (much, into if axis == "z" else into.at[0]), sems)

    xc = {}

    def swap_start(number, half):
        rows = pl.ds(half * 256, 256)
        xc[number, half] = send(
            XS.at[number, rows],
            XR.at[number, rows],
            xc_s.at[number, half],
            xc_r.at[number, half],
            sibling,
        )

    def swap_sum(number, rows):
        return XS[number, rows].astype(F32) + XR[number, rows].astype(F32)

    def swap_rows(number, make):
        for half in range(2):
            rows = slice(half * 256, half * 256 + 256)
            XS[number, rows] = make(rows).astype(BF)
            swap_start(number, half)

    def each_rows(body, size=128, start=0, stop=SEQ):
        def one(step, carry):
            body(pl.ds(pl.multiple_of(start + step * size, size), size), start + step * size)
            return carry

        lax.fori_loop(0, (stop - start) // size, one, 0)

    def norm_rows(number, rows, values):
        center = values - jnp.mean(values, -1, keepdims=True)
        inv_std = lax.rsqrt(jnp.mean(center * center, -1, keepdims=True) + EPSILON)
        x_hat = center * inv_std
        XH[number, rows] = x_hat
        IV[number, rows] = inv_std
        gain, bias = GAIN[2 * number : 2 * number + 1], GAIN[2 * number + 1 : 2 * number + 2]
        H[number, rows] = (x_hat * gain + bias).astype(BF)

    def norm_back(number, rows, grad_h):
        x_hat, inv_std = XH[number, rows], IV[number, rows]
        NGR[2 * number] += jnp.sum((grad_h * x_hat).reshape(-1, 8, WIDTH), 0)
        NGR[2 * number + 1] += jnp.sum(grad_h.reshape(-1, 8, WIDTH), 0)
        grad_hat = grad_h * GAIN[2 * number : 2 * number + 1]
        return inv_std * (
            grad_hat
            - jnp.mean(grad_hat, -1, keepdims=True)
            - x_hat * jnp.mean(grad_hat * x_hat, -1, keepdims=True)
        )

    length_n, break_n = len_ref[x], brk_ref[x]

    def live_of(places):
        linker = (places >= break_n) & (places < break_n + LINKER)
        return (places < length_n) & jnp.logical_not(linker)

    def key_fill(count):
        places = lax.broadcasted_iota(jnp.int32, (1, count), 1)
        return jnp.where(live_of(places), 0.0, NEG_FILL)

    head_of = lax.broadcasted_iota(jnp.int32, (1, COLS), 1) // HD

    def split_heads(number):
        keys, values = K[number], V[number]
        for head in range(HEADS_HERE):
            KM[number, head] = jnp.where(head_of == head, keys, jnp.zeros_like(keys))
            VM[number, head] = jnp.where(head_of == head, values, jnp.zeros_like(values))

    def attend(number, half):
        count = 256 * (half + 1) if number == 0 else SEQ
        fill = key_fill(count)

        def body(rows, first):
            bias = fill
            if number == 0:
                row = first + lax.broadcasted_iota(jnp.int32, (128, count), 0)
                col = lax.broadcasted_iota(jnp.int32, (128, count), 1)
                bias = jnp.where(col <= row, fill, NEG_FILL)
            query = Q[number, rows]
            mixed = jnp.zeros((128, COLS), F32)
            for head in range(HEADS_HERE):
                scores = nt(query, KM[number, head, :count]) + bias
                expo = jnp.exp(scores - jnp.max(scores, -1, keepdims=True))
                prob = (expo * (1.0 / jnp.sum(expo, -1, keepdims=True))).astype(BF)
                PR[number, head, rows, :count] = prob
                mixed = mixed + nn(prob, VM[number, head, :count])
            A[number, rows] = mixed.astype(BF)

        each_rows(body, start=half * 256, stop=half * 256 + 256)

    def attend_back(number, half):
        count = 256 * (half + 1) if number == 0 else SEQ

        def body(rows, first):
            grad_o = DO[rows]
            grad_q = jnp.zeros((128, COLS), F32)
            for head in range(HEADS_HERE):
                grad_p = nt(grad_o, VM[number, head, :count])
                prob = PR[number, head, rows, :count].astype(F32)
                inner = jnp.sum(prob * grad_p, -1, keepdims=True)
                grad_s = (prob * (grad_p - inner)).astype(BF)
                DS[head, rows, :count] = grad_s
                grad_q = grad_q + nn(grad_s, KM[number, head, :count])
            DQ[rows] = (grad_q * HD**-0.5).astype(BF)

        each_rows(body, start=half * 256, stop=half * 256 + 256)

    def turned_product(number, table, source, target):
        source_t = source[...].T
        for head in range(HEADS_HERE):
            part = slice(head * HD, (head + 1) * HD)
            if number == 0:
                TR[part, 0:256] = nn(source_t[part], table[head, :, 0:256]).astype(BF)
                TR[part, 256:512] = nn(
                    source_t[part, 256:512], table[head, 256:512, 256:512]
                ).astype(BF)
            else:
                TR[part] = nn(source_t[part], table[head]).astype(BF)
        target[...] = TR[...].T

    def value_back(number):
        turned_product(number, PR.at[number], DO, DV)

    def key_back(number):
        turned_product(number, DS, Q.at[number], DK)

    def norms_pass():
        for copy in nb_first:
            copy.wait_recv()
        nb_second.append(send(NB.at[:, y], NB.at[:, y], nb_s.at[nz - 1], nb_r.at[nz - 1], y_peer))

    def gains():
        nb_second[0].wait_recv()
        per_column = nz // 4
        for column in range(4):
            first = column * per_column
            total = NB[first, 0] + NB[first, 1]
            for at in range(first + 1, first + per_column):
                total = total + NB[at, 0] + NB[at, 1]
            GAIN[:, column * 128 : (column + 1) * 128] = total
        NGR[...] = jnp.zeros_like(NGR)

    def fetched():
        for fetch in fetches:
            fetch.wait()

    def first_norm():
        each_rows(lambda rows, first: norm_rows(0, rows, tok[rows].astype(F32)))
        HT[0] = H[0].T

    def cotangent_rows():
        def dead_rows(rows, first):
            places = first + lax.broadcasted_iota(jnp.int32, (128, 1), 0)
            DZ[rows] = jnp.where(live_of(places), cot[rows].astype(F32), 0.0).astype(BF)

        each_rows(dead_rows)
        HT[4] = DZ[...].T

    def memory_turned():
        HT[1] = mem[...].T

    def self_queries():
        Q[0] = (nn(H[0], weight(WQ1)) * HD**-0.5).astype(BF)
        K[0] = nn(H[0], weight(WK1)).astype(BF)

    def self_values():
        V[0] = nn(H[0], weight(WV1)).astype(BF)
        split_heads(0)

    def project(number):
        out_w = weight(WO2 if number else WO1)
        swap_rows(number, lambda rows: nt(A[number, rows], out_w))

    def memory_keys():
        K[1] = nn(mem[...], weight(WK2)).astype(BF)
        V[1] = nn(mem[...], weight(WV2)).astype(BF)
        split_heads(1)

    def swapped(number):
        xc[number, 0].wait_recv()
        xc[number, 1].wait_recv()

    def second_norm():
        def second_rows(rows, first):
            values = tok[rows].astype(F32) + swap_sum(0, rows)
            XF[rows] = values
            norm_rows(1, rows, values)

        each_rows(second_rows)

    def cross_queries():
        Q[1] = (nn(H[1], weight(WQ2)) * HD**-0.5).astype(BF)

    def turn(number):
        HT[1 + number] = H[number].T

    def third_norm():
        def third_rows(rows, first):
            values = XF[rows] + swap_sum(1, rows)
            XF[rows] = values
            norm_rows(2, rows, values)

        each_rows(third_rows)

    def hidden_chunk(chunk):
        up, down = weight(8 + 2 * chunk), weight(9 + 2 * chunk)

        def hidden_rows(rows, first):
            hidden = nn(H[2, rows], up)
            grad_act = nn(DZ[rows], down)
            gate = 0.5 + 0.5 * lax.erf(hidden * 0.5**0.5)
            slope = gate + hidden * jnp.exp(-0.5 * hidden * hidden) * 0.3989422804014327
            act = (hidden * gate).astype(BF)
            grad_u = (grad_act * slope).astype(BF)
            ACT[rows] = act
            DU[rows] = grad_u
            if chunk == 0:
                OACC[rows] = nt(act, down)
                DHA[rows] = nt(grad_u, up)
            else:
                OACC[rows] += nt(act, down)
                DHA[rows] += nt(grad_u, up)

        each_rows(hidden_rows, size=256)

    def hidden_grads(chunk):
        put_grad(8 + 2 * chunk, nn(HT[3], DU[...]))
        put_grad(9 + 2 * chunk, nn(HT[4], ACT[...]))

    def hidden_swap():
        swap_rows(3, lambda rows: DHA[rows])

    def out_swap():
        swap_rows(2, lambda rows: OACC[rows])

    def back_third():
        def one(rows, first):
            grad = DZ[rows].astype(F32) + norm_back(2, rows, swap_sum(3, rows))
            DX[rows] = grad
            H[2, rows] = grad.astype(BF)

        each_rows(one)

    def back_second():
        def one(rows, first):
            grad = DX[rows] + norm_back(1, rows, swap_sum(4, rows))
            DX[rows] = grad
            H[2, rows] = grad.astype(BF)

        each_rows(one)

    def back_first():
        def one(rows, first):
            grad = DX[rows] + norm_back(0, rows, swap_sum(5, rows))
            tgrad[x, rows] = grad.astype(BF)

        each_rows(one)

    def project_back(number):
        block = WO2 if number else WO1
        DO[...] = nn(H[2], weight(block)).astype(BF)
        put_grad(block, nn(H[2].T, A[number]))

    def cross_query_back():
        up = weight(WQ2)
        swap_rows(4, lambda rows: nt(DQ[rows], up))

    def weight_grad(block, turned, grads):
        put_grad(block, nn(HT[turned], (DQ, DK, DV)[grads][...]))

    def self_back():
        w_q, w_k, w_v = weight(WQ1), weight(WK1), weight(WV1)
        swap_rows(5, lambda rows: nt(DQ[rows], w_q) + nt(DK[rows], w_k) + nt(DV[rows], w_v))

    half_own = pl.ds(pl.multiple_of(core * 256, 256), 256)
    shares = {}

    def share_start(number):
        part = (bout, tgrad)[number].at[x, half_own]
        shares[number, 0] = send(part, part, out_s.at[number, 0], out_r.at[number, 0], x_peer)

    def share_pass(number):
        shares[number, 0].wait_recv()
        part = (bout, tgrad)[number].at[1 - x, half_own]
        shares[number, 1] = send(part, part, out_s.at[number, 1], out_r.at[number, 1], sibling)

    def share_done(number):
        shares[number, 1].wait_recv()

    def out_rows():
        def one(rows, first):
            bout[x, rows] = (XF[rows] + swap_sum(2, rows)).astype(BF)

        each_rows(one)

    norm_sends = {}

    def norm_grads_start():
        for row in range(6):
            NX[0, row : row + 1] = jnp.sum(NGR[row], 0, keepdims=True)
        NX[0, 6:8] = jnp.zeros((2, WIDTH), F32)
        norm_sends["x"] = send(NX.at[0], NX.at[1], ng_s.at[0], ng_r.at[0], x_peer)

    def norm_grads_mid():
        norm_sends["x"].wait_recv()
        NY[0] = NX[0] + NX[1]
        norm_sends["y"] = send(NY.at[0], NY.at[1], ng_s.at[1], ng_r.at[1], y_peer)

    def norm_grads_last():
        norm_sends["y"].wait_recv()
        NZB[nz - 1] = NY[0] + NY[1]
        norm_sends["z"] = [
            send(NZB.at[nz - 1], NZB.at[s - 1], ng_s.at[1 + s], ng_r.at[1 + s], z_peer[s])
            for s in range(1, nz)
        ]

    def norm_grads_done():
        total = NZB[nz - 1]
        for s in range(1, nz):
            norm_sends["z"][s - 1].wait_recv()
            total = total + NZB[s - 1]
        NT[...] = total
        column = pl.ds(pl.multiple_of(dp * rows_own // 128 * 128, 128), 128)
        nsum[...] = pltpu.roll(NT[:, column], lax.rem(128 - lane_at, 128), 1)

    def finish():
        for copy in pending:
            copy.wait_send()

    plan = (
        (gather, 0, 0), (gather, 1, 0), (norms_pass,), (gather, 14, 0), (gather, 15, 0),
        (gather, 2, 0), (gather, 3, 0), (gather, 0, 1), (gather, 1, 1), (gather, 4, 0), (gather, 5, 0),
        (gains,), (fetched,), (first_norm,),
        (gather, 2, 1), (gather, 3, 1), (gather, 0, 2), (gather, 1, 2), (gather, 14, 1), (gather, 15, 1),
        (gather, 6, 0), (gather, 7, 0), (cotangent_rows,), (memory_turned,),
        (gather, 4, 1), (gather, 5, 1), (gather, 2, 2), (gather, 3, 2), (gather, 8, 0), (gather, 9, 0),
        (gather, 0, 3), (gather, 1, 3), (self_queries,),
        (gather, 6, 1), (gather, 7, 1), (gather, 4, 2), (gather, 5, 2), (gather, 10, 0), (gather, 11, 0),
        (gather, 2, 3), (self_values,), (attend, 0, 0),
        (gather, 8, 1), (gather, 9, 1), (gather, 6, 2), (gather, 7, 2), (gather, 12, 0), (gather, 13, 0),
        (attend, 0, 1), (gather, 3, 3), (project, 0),
        (gather, 10, 1), (gather, 11, 1), (gather, 8, 2), (gather, 9, 2),
        (gather, 4, 3), (gather, 5, 3), (memory_keys,), (gather, 14, 2), (gather, 15, 2),
        (swapped, 0), (second_norm,), (gather, 12, 1), (gather, 13, 1), (gather, 10, 2), (gather, 11, 2),
        (gather, 6, 3), (cross_queries,), (attend, 1, 0), (gather, 12, 2), (gather, 13, 2),
        (attend, 1, 1), (gather, 7, 3), (project, 1), (turn, 1), (swapped, 1), (third_norm,), (turn, 2),
        (gather, 8, 3), (gather, 9, 3), (hidden_chunk, 0), (hidden_grads, 0), (total, 0, 0), (total, 1, 0),
        (gather, 10, 3), (gather, 11, 3), (hidden_chunk, 1), (hidden_grads, 1), (total, 2, 0), (total, 3, 0),
        (gather, 12, 3), (gather, 13, 3), (hidden_chunk, 2), (hidden_grads, 2), (total, 4, 0), (total, 5, 0),
        (gather, 14, 3), (gather, 15, 3), (hidden_chunk, 3), (hidden_swap,),
        (hidden_grads, 3), (total, 6, 0), (total, 7, 0), (out_swap,),
        (total, 2, 1), (total, 3, 1),
        (swapped, 3), (back_third,), (project_back, 1), (total, 8, 0),
        (total, 4, 1), (total, 5, 1), (value_back, 1), (weight_grad, WV2, 1, 2), (total, 9, 0),
        (total, 0, 1), (total, 1, 1), (attend_back, 1, 0),
        (total, 6, 1), (total, 7, 1), (total, 2, 2), (total, 3, 2), (attend_back, 1, 1),
        (cross_query_back,), (weight_grad, WQ2, 2, 0), (total, 10, 0),
        (total, 4, 2), (total, 5, 2), (total, 8, 1), (total, 0, 2), (total, 1, 2),
        (key_back, 1), (weight_grad, WK2, 1, 1), (total, 11, 0), (total, 9, 1),
        (swapped, 2), (out_rows,), (share_start, 0),
        (swapped, 4), (back_second,), (project_back, 0), (total, 12, 0),
        (total, 6, 2), (total, 7, 2), (total, 10, 1), (value_back, 0), (weight_grad, WV1, 0, 2), (total, 13, 0),
        (total, 8, 2), (total, 9, 2), (attend_back, 0, 0), (total, 11, 1), (total, 10, 2),
        (total, 12, 1), (attend_back, 0, 1), (weight_grad, WQ1, 0, 0), (total, 14, 0),
        (total, 13, 1), (total, 11, 2),
        (key_back, 0), (weight_grad, WK1, 0, 1), (total, 15, 0), (self_back,),
        (total, 12, 2), (share_pass, 0), (total, 0, 3), (total, 1, 3), (total, 2, 3), (total, 3, 3),
        (swapped, 5), (back_first,), (share_start, 1), (norm_grads_start,), (total, 14, 1), (total, 13, 2),
        (total, 4, 3), (total, 5, 3), (total, 15, 1), (norm_grads_mid,),
        (total, 6, 3), (total, 7, 3), (total, 14, 2), (norm_grads_last,),
        (total, 8, 3), (total, 9, 3), (total, 15, 2), (share_pass, 1),
        (total, 10, 3), (total, 11, 3), (total, 12, 3), (norm_grads_done,),
        (total, 13, 3), (total, 14, 3), (total, 15, 3), (share_done, 0), (share_done, 1), (finish,),
    )
    for step, *of in plan:
        step(*of)


def update(weight, grad, moment, average, rate):
    moment_new = MOMENTUM * moment + grad
    weight_new = weight - rate * (grad + MOMENTUM * moment_new)
    average_new = AVG_DECAY * average + (1.0 - AVG_DECAY) * weight_new
    return moment_new, weight_new, average_new


def update_kernel(rate_scale, gsum, nsum, tlow, *refs):
    weights, moments, averages, outs = refs[0:5], refs[5:10], refs[10:15], refs[15:]
    tgrad_out, results = outs[0], outs[1:]
    tgrad_out[...] = tlow[...].astype(F32)

    def one(which, at, grad):
        found = update(
            weights[which][at],
            grad,
            moments[which][at],
            averages[which][at],
            BASE_RATES[which] * rate_scale,
        )
        for number, value in enumerate((grad, *found)):
            results[4 * which + number][at] = value

    for block, (array, index) in enumerate(BLOCK_OF):
        at = (index,) if array < 2 else (slice(None), slice(index * 128, index * 128 + 128))
        one(array, at, gsum[block])
    wide = weights[4].shape[1]
    one(4, (slice(None), slice(None)), nsum[0:6, 0:wide])


def per_device(nz, *args):
    (tokens, memory, cotangent, lengths, breaks, attn_in, attn_out, ffn_in, ffn_out, norms) = args[:10]
    moments, averages = args[10:15], args[15:20]
    own = attn_in.shape[1]
    whole = (nz, 2, own, 128)
    vmem = pl.BlockSpec(memory_space=pltpu.VMEM)
    smem = pl.BlockSpec(memory_space=pltpu.SMEM)
    hbm = pl.BlockSpec(memory_space=pl.ANY)
    dma = pltpu.SemaphoreType.DMA

    def bf(*shape):
        return pltpu.VMEM(shape, BF)

    def f32(*shape):
        return pltpu.VMEM(shape, F32)

    def landing(parcel, phase):
        _, count, route = parcel
        sizes = {"x": 2, "y": 2, "z": nz}
        left = [axis for axis in "xyz" if axis not in route[: phase + 1]]
        senders = nz - 1 if route[phase] == "z" else 1
        sides = [2] if "x" in left else []
        rest = [sizes[axis] for axis in "zy" if axis in left]
        return bf(senders, *sides, count, *rest, own, 128)

    landings = [[landing(parcel, phase) for phase in range(3)] for parcel in SUM]
    scratch = [
        bf(SEQ, WIDTH), bf(SEQ, WIDTH), bf(SEQ, WIDTH),
        bf(2, BLOCKS, *whole), bf(2, BLOCKS, *whole),
        landings,
        f32(nz, 2, 8, 128), f32(8, 128), f32(8, WIDTH),
        f32(6, 8, WIDTH), f32(2, 8, WIDTH), f32(2, 8, WIDTH), f32(nz, 8, WIDTH),
        f32(8, WIDTH),
        bf(6, SEQ, WIDTH), bf(6, SEQ, WIDTH),
        f32(SEQ, WIDTH), f32(3, SEQ, WIDTH), f32(3, SEQ, 1),
        f32(SEQ, WIDTH), f32(SEQ, WIDTH),
        bf(3, SEQ, WIDTH), bf(5, WIDTH, SEQ),
        bf(2, SEQ, COLS), bf(2, SEQ, COLS), bf(2, SEQ, COLS),
        bf(2, HEADS_HERE, SEQ, COLS), bf(2, HEADS_HERE, SEQ, COLS),
        bf(2, HEADS_HERE, SEQ, SEQ), bf(HEADS_HERE, SEQ, SEQ),
        bf(2, SEQ, COLS), f32(SEQ, WIDTH),
        bf(SEQ, COLS), bf(SEQ, COLS), bf(SEQ, COLS),
        bf(SEQ, COLS), bf(SEQ, COLS), bf(SEQ, WIDTH), bf(SEQ, COLS), bf(COLS, SEQ),
        dma((3,)), *[dma((len(GATHER), 3))] * 2, *[dma((len(SUM), 3))] * 2,
        dma((nz,)), dma((nz,)),
        dma((6, 2)), dma((6, 2)),
        dma((nz + 1,)), dma((nz + 1,)), dma((2, 2)), dma((2, 2)),
    ]
    gsum, nsum, bout, tlow = pl.pallas_call(
        functools.partial(layer_kernel, nz),
        out_shape=(
            jax.ShapeDtypeStruct((BLOCKS, own, 128), F32),
            jax.ShapeDtypeStruct((8, 128), F32),
            jax.ShapeDtypeStruct((2, SEQ, WIDTH), BF),
            jax.ShapeDtypeStruct((2, SEQ, WIDTH), BF),
        ),
        in_specs=[hbm] * 3 + [smem] * 2 + [vmem] * 5,
        out_specs=(vmem,) * 4,
        scratch_shapes=scratch,
        compiler_params=pltpu.CompilerParams(
            collective_id=0, has_side_effects=True, vmem_limit_bytes=58 * 2**20
        ),
    )(tokens, memory, cotangent, lengths, breaks, attn_in, attn_out, ffn_in, ffn_out, norms)
    weights = (attn_in, attn_out, ffn_in, ffn_out, norms)
    rate_scale = float(lax.axis_size("dp") * tokens.shape[0]) ** -0.5
    results = pl.pallas_call(
        functools.partial(update_kernel, rate_scale),
        out_shape=(jax.ShapeDtypeStruct((2, SEQ, WIDTH), F32),)
        + tuple(jax.ShapeDtypeStruct(w.shape, F32) for w in weights for _ in range(4)),
        compiler_params=pltpu.CompilerParams(vmem_limit_bytes=32 * 2**20),
    )(gsum, nsum, tlow, *weights, *moments, *averages)
    return (bout.reshape(tokens.shape), results[0].reshape(tokens.shape), *results[1:])


def solution(mesh):
    rows, attn, ffn, norm = P("dp", None), P(None, "dp", "tensor"), P("dp", "tensor"), P(None, "dp")
    weights = (attn, attn, ffn, ffn, norm)
    return jax.shard_map(
        functools.partial(per_device, mesh.shape["dp"] // 2),
        mesh=mesh,
        in_specs=(rows, rows, rows, P("dp"), P("dp")) + weights * 3,
        out_specs=(rows, rows) + tuple(spec for spec in weights for _ in range(4)),
        check_vma=False,
    )
```

```python
import functools

import jax
import jax.numpy as jnp
from jax import lax
from jax.experimental import pallas as pl
from jax.experimental.pallas import tpu as pltpu
from jax.sharding import PartitionSpec as P

HD = 64
SEQ = 512
WIDTH = 512
LINKER = 10
EPSILON = 1e-05
NEG_FILL = -1000000000.0
MOMENTUM = 0.9
AVG_DECAY = 0.6
BASE_RATES = (0.05, 1.0, 0.05, 0.05, 0.3)

BF = jnp.bfloat16
F32 = jnp.float32
MESH = pl.DeviceIdType.MESH
HEADS_HERE = 4
COLS = 256
BLOCKS = 16
BLOCK_OF = (
    (0, 0), (0, 1), (0, 2), (1, 0),
    (0, 4), (0, 5), (0, 3), (1, 1),
    (2, 0), (3, 0), (2, 1), (3, 1),
    (2, 2), (3, 2), (2, 3), (3, 3),
)
WQ1, WK1, WV1, WO1, WK2, WV2, WQ2, WO2 = range(8)
GATHER = tuple((block, 1, ("zyx", "zxy")[block % 2]) for block in range(14)) + ((14, 1, "xyz"), (15, 1, "yxz"))
SUM = (
    (8, 1, "zxy"), (9, 1, "zxy"), (10, 1, "yzx"), (11, 1, "xyz"),
    (12, 1, "yxz"), (13, 1, "yxz"), (14, 1, "xzy"), (15, 1, "yxz"),
    (7, 1, "yzx"), (5, 1, "yxz"), (6, 1, "xyz"), (4, 1, "xyz"),
    (3, 1, "xzy"), (2, 1, "yzx"), (0, 1, "yzx"), (1, 1, "yxz"),
)


def nn(left, right):
    return jnp.dot(left, right, preferred_element_type=F32)


def nt(left, right):
    return lax.dot_general(left, right, (((1,), (1,)), ((), ())), preferred_element_type=F32)


def layer_kernel(
    nz,
    tok_hbm, mem_hbm, cot_hbm, len_ref, brk_ref, ain_hbm, aout_hbm, fin_hbm, fout_hbm, norms_hbm,
    gsum_hbm, nsum_hbm, bout_hbm, tgrad_hbm,
    gsum, nsum, bout, tgrad, ain, aout, fin, fout, norms, tok, mem, cot, W, G, R, NB, NP, GAIN, NGR, NX, NY, NZB, NT,
    XS, XR, XF, XH, IV, OACC, DHA, H, HT, Q, K, V, KM, VM, PR, DS, A, DX, DQ, DK, DV,
    ACT, DU, DZ, DO, TR,
    lsem, ag_s, ag_r, rs_s, rs_r, nb_s, nb_r, xc_s, xc_r,
    ng_s, ng_r, out_s, out_r,
):
    dp, tensor = lax.axis_index("dp"), lax.axis_index("tensor")
    z, y, x, core = dp // 2, dp % 2, tensor // 2, tensor % 2
    rows_own = ain.shape[1]
    sibling = (dp, x * 2 + 1 - core)
    x_peer = (dp, (1 - x) * 2 + core)
    y_peer = (z * 2 + 1 - y, tensor)
    z_of = [None] + [lax.rem(z + step, nz) for step in range(1, nz)]
    z_peer = [None] + [(z_of[step] * 2 + y, tensor) for step in range(1, nz)]
    pending = []

    def send(src, dst, send_sem, recv_sem, peer, alone=True):
        copy = pltpu.make_async_remote_copy(
            src, dst, send_sem, recv_sem, device_id=peer, device_id_type=MESH
        )
        copy.start()
        if alone:
            pending.append(copy)
        return copy

    barrier = pltpu.get_barrier_semaphore()
    peers = [sibling, x_peer, y_peer] + z_peer[1:]
    for peer in peers:
        pl.semaphore_signal(barrier, inc=1, device_id=peer, device_id_type=MESH)
    mine = pl.ds(pl.multiple_of(x * SEQ, SEQ), SEQ)
    moves = (
        (norms_hbm, norms), (ain_hbm, ain), (aout_hbm, aout), (fin_hbm, fin), (fout_hbm, fout),
        (tok_hbm.at[mine], tok), (mem_hbm.at[mine], mem), (cot_hbm.at[mine], cot),
    )
    fetches = []
    for number, (src, dst) in enumerate(moves):
        fetch = pltpu.make_async_copy(src, dst, lsem.at[number])
        fetch.start()
        fetches.append(fetch)
    for fetch in fetches[:5]:
        fetch.wait()

    NP[...] = jnp.zeros_like(NP)
    NP[0:6, 0:rows_own] = norms[...].astype(BF).astype(F32)
    lane_at = lax.rem(dp * rows_own, 128)
    NB[z, y] = pltpu.roll(NP[...], lane_at, 1)

    def own_block(arrays, block):
        array, index = BLOCK_OF[block]
        if array < 2:
            return arrays[array][index]
        return arrays[array][:, index * 128 : (index + 1) * 128]

    for block in range(BLOCKS):
        W[x, block, z, y] = own_block((ain, aout, fin, fout), block).astype(BF)
    pl.semaphore_wait(barrier, len(peers))

    me_of = {"x": x, "y": y, "z": z}
    flights, nb_second = {}, []

    def send_all(key, axis, pieces, whole, sems):
        if axis == "z":
            copies = [(z_of[s], s - 1, z_peer[s]) for s in range(1, nz)]
        elif axis == "y":
            copies = [(1 - y, 0, y_peer)]
        else:
            copies = [(1 - x, 0, x_peer)]
        for place, slot, peer in copies:
            send(*pieces(place, slot), *sems, peer, False)
        flights[key] = pltpu.make_async_remote_copy(
            *whole, *sems, device_id=copies[0][2], device_id_type=MESH
        )
        if key[2] == 2:
            pending.append(flights[key])

    def landed(key):
        flights[key].wait_recv()
        if key[2] < 2:
            flights[key].wait_send()

    def place_of(done, blocks):
        at = {axis: slice(None) if axis in done else me_of[axis] for axis in "xyz"}
        return at, lambda: (at["x"], blocks, at["z"], at["y"])

    def gather(parcel, phase):
        if phase > 0:
            landed(("gather", parcel, phase - 1))
        if phase == 3:
            return
        first, count, route = GATHER[parcel]
        at, where = place_of(route[:phase], pl.ds(first, count))
        part = W.at[where()]
        sems = (ag_s.at[parcel], ag_r.at[parcel, phase])
        if route[phase] == "z":
            at["z"] = pl.ds(0, nz - 1)
        much = W.at[where()]
        send_all(
            ("gather", parcel, phase), route[phase], lambda place, slot: (part, part), (much, much), sems
        )

    nb_first = [
        send(NB.at[z, y], NB.at[z, y], nb_s.at[s - 1], nb_r.at[s - 1], z_peer[s])
        for s in range(1, nz)
    ]

    def weight(block):
        return jnp.concatenate(
            [W[0, block].reshape(WIDTH, 128), W[1, block].reshape(WIDTH, 128)], axis=1
        )

    def put_grad(block, value):
        low = value.astype(BF)
        G[0, block] = low[:, :128].reshape(G.shape[2:])
        G[1, block] = low[:, 128:].reshape(G.shape[2:])

    def total(parcel, phase):
        first, count, route = SUM[parcel]
        if phase > 0:
            landed(("sum", parcel, phase - 1))
            into = R[parcel][phase - 1]
            left = [axis for axis in "xyz" if axis not in route[:phase]]
            at, _ = place_of([axis for axis in left], None)
            for number in range(count):
                for side in range(2) if "x" in left else (x,):
                    here = (side, first + number, at["z"], at["y"])
                    found = G[here].astype(F32)
                    for slot in range(nz - 1 if route[phase - 1] == "z" else 1):
                        landing = into[slot, side, number] if "x" in left else into[slot, number]
                        found = found + landing.astype(F32)
                    if phase == 3:
                        gsum[first + number] = found
                    else:
                        G[here] = found.astype(BF)
        if phase == 3:
            return
        axis, into = route[phase], R[parcel][phase]
        at, where = place_of([a for a in "xyz" if a not in route[:phase]], pl.ds(first, count))

        def pieces(place, slot):
            at[axis] = place
            return G.at[where()], into.at[slot]

        at[axis] = pl.ds(0, nz - 1) if axis == "z" else me_of[axis]
        much = G.at[where()]
        sems = (rs_s.at[parcel], rs_r.at[parcel, phase])
        send_all(("sum", parcel, phase), axis, pieces, (much, into if axis == "z" else into.at[0]), sems)

    xc = {}

    def swap_start(number, half):
        rows = pl.ds(half * 256, 256)
        xc[number, half] = send(
            XS.at[number, rows],
            XR.at[number, rows],
            xc_s.at[number, half],
            xc_r.at[number, half],
            sibling,
        )

    def swap_sum(number, rows):
        return XS[number, rows].astype(F32) + XR[number, rows].astype(F32)

    def swap_rows(number, make):
        for half in range(2):
            rows = slice(half * 256, half * 256 + 256)
            XS[number, rows] = make(rows).astype(BF)
            swap_start(number, half)

    def each_rows(body, swap=None):
        for first in range(0, SEQ, 128):
            if swap is not None and first % 256 == 0:
                xc[swap, first // 256].wait_recv()
            body(slice(first, first + 128), first)

    def norm_rows(number, rows, values):
        center = values - jnp.mean(values, -1, keepdims=True)
        inv_std = lax.rsqrt(jnp.mean(center * center, -1, keepdims=True) + EPSILON)
        x_hat = center * inv_std
        XH[number, rows] = x_hat
        IV[number, rows] = inv_std
        gain, bias = GAIN[2 * number : 2 * number + 1], GAIN[2 * number + 1 : 2 * number + 2]
        H[number, rows] = (x_hat * gain + bias).astype(BF)

    def norm_back(number, rows, grad_h):
        x_hat, inv_std = XH[number, rows], IV[number, rows]
        NGR[2 * number] += jnp.sum((grad_h * x_hat).reshape(-1, 8, WIDTH), 0)
        NGR[2 * number + 1] += jnp.sum(grad_h.reshape(-1, 8, WIDTH), 0)
        grad_hat = grad_h * GAIN[2 * number : 2 * number + 1]
        return inv_std * (
            grad_hat
            - jnp.mean(grad_hat, -1, keepdims=True)
            - x_hat * jnp.mean(grad_hat * x_hat, -1, keepdims=True)
        )

    length_n, break_n = len_ref[x], brk_ref[x]

    def live_of(places):
        linker = (places >= break_n) & (places < break_n + LINKER)
        return (places < length_n) & jnp.logical_not(linker)

    def key_fill(count):
        places = lax.broadcasted_iota(jnp.int32, (1, count), 1)
        return jnp.where(live_of(places), 0.0, NEG_FILL)

    head_of = lax.broadcasted_iota(jnp.int32, (1, COLS), 1) // HD

    def split_heads(number):
        keys, values = K[number], V[number]
        for head in range(HEADS_HERE):
            KM[number, head] = jnp.where(head_of == head, keys, jnp.zeros_like(keys))
            VM[number, head] = jnp.where(head_of == head, values, jnp.zeros_like(values))

    def attend(number, half):
        count = 256 * (half + 1) if number == 0 else SEQ
        rows = slice(half * 256, half * 256 + 256)
        bias = key_fill(count)
        if number == 0:
            row = half * 256 + lax.broadcasted_iota(jnp.int32, (256, count), 0)
            col = lax.broadcasted_iota(jnp.int32, (256, count), 1)
            bias = jnp.where(col <= row, bias, NEG_FILL)
        query = Q[number, rows]
        mixed = jnp.zeros((256, COLS), F32)
        for head in range(HEADS_HERE):
            scores = nt(query, KM[number, head, :count]) + bias
            expo = jnp.exp(scores - jnp.max(scores, -1, keepdims=True))
            prob = (expo * (1.0 / jnp.sum(expo, -1, keepdims=True))).astype(BF)
            PR[number, head, rows, :count] = prob
            mixed = mixed + nn(prob, VM[number, head, :count])
        A[number, rows] = mixed.astype(BF)

    def attend_back(number, half):
        count = 256 * (half + 1) if number == 0 else SEQ
        rows = slice(half * 256, half * 256 + 256)
        grad_o = DO[rows]
        grad_q = jnp.zeros((256, COLS), F32)
        for head in range(HEADS_HERE):
            grad_p = nt(grad_o, VM[number, head, :count])
            prob = PR[number, head, rows, :count].astype(F32)
            inner = jnp.sum(prob * grad_p, -1, keepdims=True)
            grad_s = (prob * (grad_p - inner)).astype(BF)
            DS[head, rows, :count] = grad_s
            grad_q = grad_q + nn(grad_s, KM[number, head, :count])
        DQ[rows] = (grad_q * HD**-0.5).astype(BF)

    def turned_product(number, table, source, target):
        source_t = source[...].T
        for head in range(HEADS_HERE):
            part = slice(head * HD, (head + 1) * HD)
            if number == 0:
                TR[part, 0:256] = nn(source_t[part], table[head, :, 0:256]).astype(BF)
                TR[part, 256:512] = nn(
                    source_t[part, 256:512], table[head, 256:512, 256:512]
                ).astype(BF)
            else:
                TR[part] = nn(source_t[part], table[head]).astype(BF)
        target[...] = TR[...].T

    def value_back(number):
        turned_product(number, PR.at[number], DO, DV)

    def key_back(number):
        turned_product(number, DS, Q.at[number], DK)

    def norms_pass():
        for copy in nb_first:
            copy.wait_recv()
        nb_second.append(send(NB.at[:, y], NB.at[:, y], nb_s.at[nz - 1], nb_r.at[nz - 1], y_peer))

    def gains():
        nb_second[0].wait_recv()
        per_column = nz // 4
        for column in range(4):
            first = column * per_column
            total = NB[first, 0] + NB[first, 1]
            for at in range(first + 1, first + per_column):
                total = total + NB[at, 0] + NB[at, 1]
            GAIN[:, column * 128 : (column + 1) * 128] = total
        NGR[...] = jnp.zeros_like(NGR)

    def fetched():
        for fetch in fetches[5:]:
            fetch.wait()

    def first_norm():
        each_rows(lambda rows, first: norm_rows(0, rows, tok[rows].astype(F32)))

    def cotangent_rows():
        def dead_rows(rows, first):
            places = first + lax.broadcasted_iota(jnp.int32, (128, 1), 0)
            DZ[rows] = jnp.where(live_of(places), cot[rows].astype(F32), 0.0).astype(BF)

        each_rows(dead_rows)
        HT[4] = DZ[...].T

    def memory_turned():
        HT[1] = mem[...].T

    def self_queries():
        Q[0] = (nn(H[0], weight(WQ1)) * HD**-0.5).astype(BF)
        K[0] = nn(H[0], weight(WK1)).astype(BF)

    def self_values():
        V[0] = nn(H[0], weight(WV1)).astype(BF)
        split_heads(0)

    def project(number):
        out_w = weight(WO2 if number else WO1)
        swap_rows(number, lambda rows: nt(A[number, rows], out_w))

    def memory_keys():
        K[1] = nn(mem[...], weight(WK2)).astype(BF)
        V[1] = nn(mem[...], weight(WV2)).astype(BF)
        split_heads(1)

    def second_norm():
        def second_rows(rows, first):
            values = tok[rows].astype(F32) + swap_sum(0, rows)
            XF[rows] = values
            norm_rows(1, rows, values)

        each_rows(second_rows, 0)

    def cross_queries():
        Q[1] = (nn(H[1], weight(WQ2)) * HD**-0.5).astype(BF)

    def turn(number):
        HT[number + 1 if number else 0] = H[number].T

    def third_norm():
        def third_rows(rows, first):
            values = XF[rows] + swap_sum(1, rows)
            XF[rows] = values
            norm_rows(2, rows, values)

        each_rows(third_rows, 1)

    def hidden_chunk(chunk):
        up, down = weight(8 + 2 * chunk), weight(9 + 2 * chunk)

        def hidden_rows(rows, first):
            hidden = nn(H[2, rows], up)
            grad_act = nn(DZ[rows], down)
            gate = 0.5 + 0.5 * lax.erf(hidden * 0.5**0.5)
            slope = gate + hidden * jnp.exp(-0.5 * hidden * hidden) * 0.3989422804014327
            act = (hidden * gate).astype(BF)
            grad_u = (grad_act * slope).astype(BF)
            ACT[rows] = act
            DU[rows] = grad_u
            if chunk == 0:
                OACC[rows] = nt(act, down)
                DHA[rows] = nt(grad_u, up)
            else:
                OACC[rows] += nt(act, down)
                DHA[rows] += nt(grad_u, up)

        for half in range(2):
            hidden_rows(slice(half * 256, half * 256 + 256), half * 256)

    def hidden_grads(chunk):
        put_grad(8 + 2 * chunk, nn(HT[3], DU[...]))
        put_grad(9 + 2 * chunk, nn(HT[4], ACT[...]))

    def hidden_swap():
        swap_rows(3, lambda rows: DHA[rows])

    def out_swap():
        swap_rows(2, lambda rows: OACC[rows])

    def back_third():
        def one(rows, first):
            grad = DZ[rows].astype(F32) + norm_back(2, rows, swap_sum(3, rows))
            DX[rows] = grad
            H[2, rows] = grad.astype(BF)

        each_rows(one, 3)

    def back_second():
        def one(rows, first):
            grad = DX[rows] + norm_back(1, rows, swap_sum(4, rows))
            DX[rows] = grad
            H[2, rows] = grad.astype(BF)

        each_rows(one, 4)

    def back_first():
        def one(rows, first):
            grad = DX[rows] + norm_back(0, rows, swap_sum(5, rows))
            tgrad[x, rows] = grad.astype(BF)

        each_rows(one, 5)

    def project_back(number):
        block = WO2 if number else WO1
        DO[...] = nn(H[2], weight(block)).astype(BF)
        put_grad(block, nn(H[2].T, A[number]))

    def cross_query_back():
        up = weight(WQ2)
        swap_rows(4, lambda rows: nt(DQ[rows], up))

    def weight_grad(block, turned, grads):
        put_grad(block, nn(HT[turned], (DQ, DK, DV)[grads][...]))

    def self_back():
        w_q, w_k, w_v = weight(WQ1), weight(WK1), weight(WV1)
        swap_rows(5, lambda rows: nt(DQ[rows], w_q) + nt(DK[rows], w_k) + nt(DV[rows], w_v))

    half_own = pl.ds(pl.multiple_of(core * 256, 256), 256)
    shares = {}

    def share_start(number):
        part = (bout, tgrad)[number].at[x, half_own]
        shares[number, 0] = send(part, part, out_s.at[number, 0], out_r.at[number, 0], x_peer)

    def share_pass(number):
        shares[number, 0].wait_recv()
        part = (bout, tgrad)[number].at[1 - x, half_own]
        shares[number, 1] = send(part, part, out_s.at[number, 1], out_r.at[number, 1], sibling)

    def share_done(number):
        shares[number, 1].wait_recv()
        store((bout, tgrad)[number], (bout_hbm, tgrad_hbm)[number])

    def out_rows():
        def one(rows, first):
            bout[x, rows] = (XF[rows] + swap_sum(2, rows)).astype(BF)

        each_rows(one, 2)

    norm_sends = {}

    def norm_grads_start():
        for row in range(6):
            NX[0, row : row + 1] = jnp.sum(NGR[row], 0, keepdims=True)
        NX[0, 6:8] = jnp.zeros((2, WIDTH), F32)
        norm_sends["x"] = send(NX.at[0], NX.at[1], ng_s.at[0], ng_r.at[0], x_peer)

    def norm_grads_mid():
        norm_sends["x"].wait_recv()
        NY[0] = NX[0] + NX[1]
        norm_sends["y"] = send(NY.at[0], NY.at[1], ng_s.at[1], ng_r.at[1], y_peer)

    def norm_grads_last():
        norm_sends["y"].wait_recv()
        NZB[nz - 1] = NY[0] + NY[1]
        norm_sends["z"] = [
            send(NZB.at[nz - 1], NZB.at[s - 1], ng_s.at[1 + s], ng_r.at[1 + s], z_peer[s])
            for s in range(1, nz)
        ]

    def norm_grads_done():
        total = NZB[nz - 1]
        for s in range(1, nz):
            norm_sends["z"][s - 1].wait_recv()
            total = total + NZB[s - 1]
        NT[...] = total
        column = pl.ds(pl.multiple_of(dp * rows_own // 128 * 128, 128), 128)
        nsum[...] = pltpu.roll(NT[:, column], lax.rem(128 - lane_at, 128), 1)

    stored = []

    def store(src, dst):
        copy = pltpu.make_async_copy(src, dst, lsem.at[8 + len(stored)])
        copy.start()
        stored.append(copy)

    def finish():
        store(gsum, gsum_hbm)
        store(nsum, nsum_hbm)
        for copy in pending:
            copy.wait_send()
        for copy in stored:
            copy.wait()

    plan = ((gather,0,0,),(gather,1,0,),(gather,2,0,),(gather,4,0,),(gather,3,0,),(gather,5,0,),(gather,14,0,),(gather,15,0,),(fetched,),(memory_turned,),(cotangent_rows,),(norms_pass,),(gather,6,0,),(gather,0,1,),(gather,7,0,),(gather,14,1,),(gather,15,1,),(gains,),(gather,1,1,),(gather,8,0,),(first_norm,),(turn,0,),(gather,2,1,),(gather,9,0,),(gather,0,2,),(gather,4,1,),(gather,14,2,),(gather,1,2,),(gather,3,1,),(gather,2,2,),(gather,5,1,),(gather,4,2,),(gather,0,3,),(gather,6,1,),(gather,7,1,),(gather,3,2,),(gather,11,0,),(gather,1,3,),(self_queries,),(gather,8,1,),(gather,10,0,),(gather,6,2,),(gather,2,3,),(self_values,),(attend,0,0,),(gather,9,1,),(gather,13,0,),(gather,3,3,),(gather,5,2,),(gather,12,0,),(attend,0,1,),(gather,15,2,),(gather,4,3,),(gather,8,2,),(gather,14,3,),(project,0,),(gather,7,2,),(gather,11,1,),(gather,5,3,),(memory_keys,),(second_norm,),(gather,6,3,),(cross_queries,),(gather,10,1,),(attend,1,0,),(gather,13,1,),(gather,9,2,),(gather,7,3,),(gather,12,1,),(attend,1,1,),(gather,8,3,),(gather,10,2,),(project,1,),(gather,11,2,),(turn,1,),(gather,9,3,),(gather,13,2,),(third_norm,),(gather,15,3,),(gather,12,2,),(turn,2,),(hidden_chunk,0,),(gather,10,3,),(hidden_grads,0,),(total,0,0,),(gather,11,3,),(hidden_chunk,1,),(hidden_grads,1,),(total,2,0,),(total,3,0,),(total,1,0,),(gather,12,3,),(gather,13,3,),(hidden_chunk,2,),(hidden_grads,2,),(total,4,0,),(total,5,0,),(hidden_chunk,3,),(hidden_swap,),(out_swap,),(hidden_grads,3,),(total,6,0,),(total,3,1,),(total,2,1,),(total,0,1,),(total,7,0,),(back_third,),(out_rows,),(share_start,0,),(project_back,1,),(attend_back,1,0,),(total,8,0,),(total,6,1,),(total,4,1,),(attend_back,1,1,),(total,3,2,),(total,0,2,),(total,5,1,),(value_back,1,),(total,1,1,),(total,2,2,),(weight_grad,WV2,1,2,),(total,9,0,),(total,7,1,),(cross_query_back,),(share_pass,0,),(weight_grad,WQ2,2,0,),(total,10,0,),(key_back,1,),(total,6,2,),(total,4,2,),(total,8,1,),(share_done,0,),(back_second,),(total,5,2,),(project_back,0,),(total,1,2,),(total,9,1,),(total,12,0,),(attend_back,0,0,),(total,7,2,),(value_back,0,),(weight_grad,WV1,0,2,),(total,13,0,),(attend_back,0,1,),(total,8,2,),(total,10,1,),(weight_grad,WK2,1,1,),(total,11,0,),(total,9,2,),(key_back,0,),(self_back,),(weight_grad,WQ1,0,0,),(total,14,0,),(total,12,1,),(total,13,1,),(weight_grad,WK1,0,1,),(total,15,0,),(total,4,3,),(back_first,),(share_start,1,),(total,9,3,),(total,10,2,),(norm_grads_start,),(total,11,1,),(total,2,3,),(total,3,3,),(total,8,3,),(total,6,3,),(total,5,3,),(total,0,3,),(total,7,3,),(total,1,3,),(total,14,1,),(total,12,2,),(total,15,1,),(total,13,2,),(total,11,2,),(total,12,3,),(total,10,3,),(share_pass,1,),(norm_grads_mid,),(total,15,2,),(total,13,3,),(share_done,1,),(norm_grads_last,),(total,14,2,),(total,11,3,),(total,14,3,),(total,15,3,),(norm_grads_done,),(finish,),)
    for step, *of in plan:
        step(*of)


def update(weight, grad, moment, average, rate):
    moment_new = MOMENTUM * moment + grad
    weight_new = weight - rate * (grad + MOMENTUM * moment_new)
    average_new = AVG_DECAY * average + (1.0 - AVG_DECAY) * weight_new
    return moment_new, weight_new, average_new


def update_kernel(rate_scale, gsum_hbm, nsum_hbm, tlow_hbm, bout_hbm, *refs):
    sources, targets = refs[0:15], refs[15:37]
    gsum, nsum, tlow, bout, tgrad, *held, in_sems, out_sems = refs[37:]
    fetched, results = held[0:15], held[15:35]
    moves = (
        (tlow_hbm, tlow), (bout_hbm, bout), (gsum_hbm, gsum), (nsum_hbm, nsum),
        *zip(sources, fetched),
    )
    fetches = [
        pltpu.make_async_copy(src, dst, in_sems.at[number])
        for number, (src, dst) in enumerate(moves)
    ]
    for fetch in fetches:
        fetch.start()
    stores = []

    def store(src, number):
        copy = pltpu.make_async_copy(src, targets[number], out_sems.at[number])
        copy.start()
        stores.append(copy)

    fetches[0].wait()
    tgrad[...] = tlow[...].astype(F32)
    store(tgrad, 1)
    fetches[1].wait()
    store(bout, 0)
    fetches[2].wait()
    fetches[3].wait()
    for which in range(5):
        weight, moment, average = fetched[which], fetched[5 + which], fetched[10 + which]
        for turn in range(3):
            fetches[4 + 5 * turn + which].wait()
        if which < 4:
            parts = [
                ((index,) if which < 2 else (slice(None), slice(index * 128, index * 128 + 128)), gsum[block])
                for block, (array, index) in enumerate(BLOCK_OF)
                if array == which
            ]
        else:
            parts = [((slice(None), slice(None)), nsum[0:6, 0 : weight.shape[1]])]
        for at, grad in parts:
            rate = BASE_RATES[which] * rate_scale
            found = update(weight[at], grad, moment[at], average[at], rate)
            for number, value in enumerate((grad, *found)):
                results[4 * which + number][at] = value
        for number in range(4):
            store(results[4 * which + number], 2 + 4 * which + number)
    for copy in stores:
        copy.wait()


def per_device(nz, *args):
    (tokens, memory, cotangent, lengths, breaks, attn_in, attn_out, ffn_in, ffn_out, norms) = args[:10]
    moments, averages = args[10:15], args[15:20]
    own = attn_in.shape[1]
    whole = (nz, 2, own, 128)
    smem = pl.BlockSpec(memory_space=pltpu.SMEM)
    hbm = pl.BlockSpec(memory_space=pl.ANY)
    dma = pltpu.SemaphoreType.DMA

    def bf(*shape):
        return pltpu.VMEM(shape, BF)

    def f32(*shape):
        return pltpu.VMEM(shape, F32)

    def landing(parcel, phase):
        _, count, route = parcel
        sizes = {"x": 2, "y": 2, "z": nz}
        left = [axis for axis in "xyz" if axis not in route[: phase + 1]]
        senders = nz - 1 if route[phase] == "z" else 1
        sides = [2] if "x" in left else []
        rest = [sizes[axis] for axis in "zy" if axis in left]
        return bf(senders, *sides, count, *rest, own, 128)

    landings = [[landing(parcel, phase) for phase in range(3)] for parcel in SUM]
    scratch = [
        f32(BLOCKS, own, 128), f32(8, 128), bf(2, SEQ, WIDTH), bf(2, SEQ, WIDTH),
        *[f32(*array.shape) for array in (attn_in, attn_out, ffn_in, ffn_out, norms)],
        bf(SEQ, WIDTH), bf(SEQ, WIDTH), bf(SEQ, WIDTH),
        bf(2, BLOCKS, *whole), bf(2, BLOCKS, *whole),
        landings,
        f32(nz, 2, 8, 128), f32(8, 128), f32(8, WIDTH),
        f32(6, 8, WIDTH), f32(2, 8, WIDTH), f32(2, 8, WIDTH), f32(nz, 8, WIDTH),
        f32(8, WIDTH),
        bf(6, SEQ, WIDTH), bf(6, SEQ, WIDTH),
        f32(SEQ, WIDTH), f32(3, SEQ, WIDTH), f32(3, SEQ, 1),
        f32(SEQ, WIDTH), f32(SEQ, WIDTH),
        bf(3, SEQ, WIDTH), bf(5, WIDTH, SEQ),
        bf(2, SEQ, COLS), bf(2, SEQ, COLS), bf(2, SEQ, COLS),
        bf(2, HEADS_HERE, SEQ, COLS), bf(2, HEADS_HERE, SEQ, COLS),
        bf(2, HEADS_HERE, SEQ, SEQ), bf(HEADS_HERE, SEQ, SEQ),
        bf(2, SEQ, COLS), f32(SEQ, WIDTH),
        bf(SEQ, COLS), bf(SEQ, COLS), bf(SEQ, COLS),
        bf(SEQ, COLS), bf(SEQ, COLS), bf(SEQ, WIDTH), bf(SEQ, COLS), bf(COLS, SEQ),
        dma((12,)), dma((len(GATHER),)), dma((len(GATHER), 3)),
        dma((len(SUM),)), dma((len(SUM), 3)),
        dma((nz,)), dma((nz,)),
        dma((6, 2)), dma((6, 2)),
        dma((nz + 1,)), dma((nz + 1,)), dma((2, 2)), dma((2, 2)),
    ]
    gsum, nsum, bout, tlow = pl.pallas_call(
        functools.partial(layer_kernel, nz),
        out_shape=(
            jax.ShapeDtypeStruct((BLOCKS, own, 128), F32),
            jax.ShapeDtypeStruct((8, 128), F32),
            jax.ShapeDtypeStruct((2, SEQ, WIDTH), BF),
            jax.ShapeDtypeStruct((2, SEQ, WIDTH), BF),
        ),
        in_specs=[hbm] * 3 + [smem] * 2 + [hbm] * 5,
        out_specs=(hbm,) * 4,
        scratch_shapes=scratch,
        compiler_params=pltpu.CompilerParams(
            collective_id=0, has_side_effects=True, vmem_limit_bytes=58 * 2**20
        ),
    )(tokens, memory, cotangent, lengths, breaks, attn_in, attn_out, ffn_in, ffn_out, norms)
    weights = (attn_in, attn_out, ffn_in, ffn_out, norms)
    rate_scale = float(lax.axis_size("dp") * tokens.shape[0]) ** -0.5
    results = pl.pallas_call(
        functools.partial(update_kernel, rate_scale),
        out_shape=(
            jax.ShapeDtypeStruct((2, SEQ, WIDTH), BF),
            jax.ShapeDtypeStruct((2, SEQ, WIDTH), F32),
            *[jax.ShapeDtypeStruct(w.shape, F32) for w in weights for _ in range(4)],
        ),
        in_specs=[hbm] * 19,
        out_specs=(hbm,) * 22,
        scratch_shapes=[
            f32(BLOCKS, own, 128), f32(8, 128), bf(2, SEQ, WIDTH), bf(2, SEQ, WIDTH), f32(2, SEQ, WIDTH),
            *[f32(*w.shape) for w in (*weights, *moments, *averages)],
            *[f32(*w.shape) for w in weights for _ in range(4)],
            dma((19,)), dma((22,)),
        ],
        compiler_params=pltpu.CompilerParams(vmem_limit_bytes=63 * 2**20),
    )(gsum, nsum, tlow, bout, *weights, *moments, *averages)
    return (results[0].reshape(tokens.shape), results[1].reshape(tokens.shape), *results[2:])


def solution(mesh):
    rows, attn, ffn, norm = P("dp", None), P(None, "dp", "tensor"), P("dp", "tensor"), P(None, "dp")
    weights = (attn, attn, ffn, ffn, norm)
    return jax.shard_map(
        functools.partial(per_device, mesh.shape["dp"] // 2),
        mesh=mesh,
        in_specs=(rows, rows, rows, P("dp"), P("dp")) + weights * 3,
        out_specs=(rows, rows) + tuple(spec for spec in weights for _ in range(4)),
        check_vma=False,
    )
```

```python
import functools

import jax
import jax.numpy as jnp
from jax import lax
from jax.experimental import pallas as pl
from jax.experimental.pallas import tpu as pltpu
from jax.sharding import PartitionSpec as P

HD = 64
SEQ = 512
WIDTH = 512
LINKER = 10
EPSILON = 1e-05
NEG_FILL = -1000000000.0
MOMENTUM = 0.9
AVG_DECAY = 0.6
BASE_RATES = (0.05, 1.0, 0.05, 0.05, 0.3)

BF = jnp.bfloat16
F32 = jnp.float32
MESH = pl.DeviceIdType.MESH
HEADS_HERE = 4
COLS = 256
BLOCKS = 16
BLOCK_OF = (
    (0, 0), (0, 1), (0, 2), (1, 0),
    (0, 4), (0, 5), (0, 3), (1, 1),
    (2, 0), (3, 0), (2, 1), (3, 1),
    (2, 2), (3, 2), (2, 3), (3, 3),
)
WQ1, WK1, WV1, WO1, WK2, WV2, WQ2, WO2 = range(8)
GATHER = tuple((block, 1, ("zyx", "zxy")[block % 2]) for block in range(14)) + ((14, 1, "xyz"), (15, 1, "yxz"))
SUM = (
    (8, 1, "xyz"), (9, 1, "zxy"), (10, 1, "yxz"), (11, 1, "xyz"),
    (12, 1, "xyz"), (13, 1, "xyz"), (14, 1, "yzx"), (15, 1, "zyx"),
    (7, 1, "zxy"), (5, 1, "xyz"), (6, 1, "yxz"), (4, 1, "yzx"),
    (3, 1, "yxz"), (2, 1, "yzx"), (0, 1, "xyz"), (1, 1, "xyz"),
)


def nn(left, right):
    return jnp.dot(left, right, preferred_element_type=F32)


def nt(left, right):
    return lax.dot_general(left, right, (((1,), (1,)), ((), ())), preferred_element_type=F32)


def layer_kernel(
    nz,
    tok_hbm, mem_hbm, cot_hbm, len_ref, brk_ref, ain_hbm, aout_hbm, fin_hbm, fout_hbm, norms_hbm,
    gsum_hbm, nsum_hbm, bout_hbm, tgrad_hbm,
    gsum, nsum, bout, tgrad, ain, aout, fin, fout, norms, tok, mem, cot, W, G, R, NB, NP, GAIN, NGR, NX, NY, NZB, NT,
    XS, XR, XF, XH, IV, OACC, DHA, H, HT, Q, K, V, KM, VM, PR, DS, A, DX, DQ, DK, DV,
    ACT, DU, DZ, DO, TR,
    lsem, ag_s, ag_r, rs_s, rs_r, nb_s, nb_r, xc_s, xc_r,
    ng_s, ng_r, out_s, out_r,
):
    dp, tensor = lax.axis_index("dp"), lax.axis_index("tensor")
    z, y, x, core = dp // 2, dp % 2, tensor // 2, tensor % 2
    rows_own = ain.shape[1]
    sibling = (dp, x * 2 + 1 - core)
    x_peer = (dp, (1 - x) * 2 + core)
    y_peer = (z * 2 + 1 - y, tensor)
    z_of = [None] + [lax.rem(z + step, nz) for step in range(1, nz)]
    z_peer = [None] + [(z_of[step] * 2 + y, tensor) for step in range(1, nz)]
    pending = []

    def send(src, dst, send_sem, recv_sem, peer, alone=True):
        copy = pltpu.make_async_remote_copy(
            src, dst, send_sem, recv_sem, device_id=peer, device_id_type=MESH
        )
        copy.start()
        if alone:
            pending.append(copy)
        return copy

    barrier = pltpu.get_barrier_semaphore()
    peers = [sibling, x_peer, y_peer] + z_peer[1:]
    for peer in peers:
        pl.semaphore_signal(barrier, inc=1, device_id=peer, device_id_type=MESH)
    mine = pl.ds(pl.multiple_of(x * SEQ, SEQ), SEQ)
    moves = (
        (norms_hbm, norms), (ain_hbm, ain), (aout_hbm, aout), (fin_hbm, fin), (fout_hbm, fout),
        (tok_hbm.at[mine], tok), (mem_hbm.at[mine], mem), (cot_hbm.at[mine], cot),
    )
    fetches = []
    for number, (src, dst) in enumerate(moves):
        fetch = pltpu.make_async_copy(src, dst, lsem.at[number])
        fetch.start()
        fetches.append(fetch)
    for fetch in fetches[:5]:
        fetch.wait()

    NP[...] = jnp.zeros_like(NP)
    NP[0:6, 0:rows_own] = norms[...].astype(BF).astype(F32)
    lane_at = lax.rem(dp * rows_own, 128)
    NB[z, y] = pltpu.roll(NP[...], lane_at, 1)

    def own_block(arrays, block):
        array, index = BLOCK_OF[block]
        if array < 2:
            return arrays[array][index]
        return arrays[array][:, index * 128 : (index + 1) * 128]

    for block in range(BLOCKS):
        W[x, block, z, y] = own_block((ain, aout, fin, fout), block).astype(BF)
    pl.semaphore_wait(barrier, len(peers))

    me_of = {"x": x, "y": y, "z": z}
    flights, nb_second = {}, []

    def send_all(key, axis, pieces, whole, sems):
        if axis == "z":
            copies = [(z_of[s], s - 1, z_peer[s]) for s in range(1, nz)]
        elif axis == "y":
            copies = [(1 - y, 0, y_peer)]
        else:
            copies = [(1 - x, 0, x_peer)]
        for place, slot, peer in copies:
            send(*pieces(place, slot), *sems, peer, False)
        flights[key] = pltpu.make_async_remote_copy(
            *whole, *sems, device_id=copies[0][2], device_id_type=MESH
        )
        if key[2] == 2:
            pending.append(flights[key])

    def landed(key):
        flights[key].wait_recv()
        if key[2] < 2:
            flights[key].wait_send()

    def place_of(done, blocks):
        at = {axis: slice(None) if axis in done else me_of[axis] for axis in "xyz"}
        return at, lambda: (at["x"], blocks, at["z"], at["y"])

    def gather(parcel, phase):
        if phase > 0:
            landed(("gather", parcel, phase - 1))
        if phase == 3:
            return
        first, count, route = GATHER[parcel]
        at, where = place_of(route[:phase], pl.ds(first, count))
        part = W.at[where()]
        sems = (ag_s.at[parcel], ag_r.at[parcel, phase])
        if route[phase] == "z":
            at["z"] = pl.ds(0, nz - 1)
        much = W.at[where()]
        send_all(
            ("gather", parcel, phase), route[phase], lambda place, slot: (part, part), (much, much), sems
        )

    nb_first = [
        send(NB.at[z, y], NB.at[z, y], nb_s.at[s - 1], nb_r.at[s - 1], z_peer[s])
        for s in range(1, nz)
    ]

    def weight(block):
        return jnp.concatenate(
            [W[0, block].reshape(WIDTH, 128), W[1, block].reshape(WIDTH, 128)], axis=1
        )

    def put_grad(block, value):
        low = value.astype(BF)
        G[0, block] = low[:, :128].reshape(G.shape[2:])
        G[1, block] = low[:, 128:].reshape(G.shape[2:])

    def total(parcel, phase):
        first, count, route = SUM[parcel]
        if phase > 0:
            landed(("sum", parcel, phase - 1))
            into = R[parcel][phase - 1]
            left = [axis for axis in "xyz" if axis not in route[:phase]]
            at, _ = place_of([axis for axis in left], None)
            for number in range(count):
                for side in range(2) if "x" in left else (x,):
                    here = (side, first + number, at["z"], at["y"])
                    found = G[here].astype(F32)
                    for slot in range(nz - 1 if route[phase - 1] == "z" else 1):
                        landing = into[slot, side, number] if "x" in left else into[slot, number]
                        found = found + landing.astype(F32)
                    if phase == 3:
                        gsum[first + number] = found
                    else:
                        G[here] = found.astype(BF)
        if phase == 3:
            return
        axis, into = route[phase], R[parcel][phase]
        at, where = place_of([a for a in "xyz" if a not in route[:phase]], pl.ds(first, count))

        def pieces(place, slot):
            at[axis] = place
            return G.at[where()], into.at[slot]

        at[axis] = pl.ds(0, nz - 1) if axis == "z" else me_of[axis]
        much = G.at[where()]
        sems = (rs_s.at[parcel], rs_r.at[parcel, phase])
        send_all(("sum", parcel, phase), axis, pieces, (much, into if axis == "z" else into.at[0]), sems)

    xc = {}

    def swap_start(number, half):
        rows = pl.ds(half * 256, 256)
        xc[number, half] = send(
            XS.at[number, rows],
            XR.at[number, rows],
            xc_s.at[number, half],
            xc_r.at[number, half],
            sibling,
        )

    def swap_sum(number, rows):
        return XS[number, rows].astype(F32) + XR[number, rows].astype(F32)

    def swap_rows(number, make):
        for half in range(2):
            rows = slice(half * 256, half * 256 + 256)
            XS[number, rows] = make(rows).astype(BF)
            swap_start(number, half)

    def each_rows(body, swap=None):
        for first in range(0, SEQ, 128):
            if swap is not None and first % 256 == 0:
                xc[swap, first // 256].wait_recv()
            body(slice(first, first + 128), first)

    def norm_rows(number, rows, values):
        center = values - jnp.mean(values, -1, keepdims=True)
        inv_std = lax.rsqrt(jnp.mean(center * center, -1, keepdims=True) + EPSILON)
        x_hat = center * inv_std
        XH[number, rows] = x_hat
        IV[number, rows] = inv_std
        gain, bias = GAIN[2 * number : 2 * number + 1], GAIN[2 * number + 1 : 2 * number + 2]
        H[number, rows] = (x_hat * gain + bias).astype(BF)

    def norm_back(number, rows, grad_h):
        x_hat, inv_std = XH[number, rows], IV[number, rows]
        NGR[2 * number] += jnp.sum((grad_h * x_hat).reshape(-1, 8, WIDTH), 0)
        NGR[2 * number + 1] += jnp.sum(grad_h.reshape(-1, 8, WIDTH), 0)
        grad_hat = grad_h * GAIN[2 * number : 2 * number + 1]
        return inv_std * (
            grad_hat
            - jnp.mean(grad_hat, -1, keepdims=True)
            - x_hat * jnp.mean(grad_hat * x_hat, -1, keepdims=True)
        )

    length_n, break_n = len_ref[x], brk_ref[x]

    def live_of(places):
        linker = (places >= break_n) & (places < break_n + LINKER)
        return (places < length_n) & jnp.logical_not(linker)

    def key_fill(count):
        places = lax.broadcasted_iota(jnp.int32, (1, count), 1)
        return jnp.where(live_of(places), 0.0, NEG_FILL)

    head_of = lax.broadcasted_iota(jnp.int32, (1, COLS), 1) // HD

    def split_heads(number):
        keys, values = K[number], V[number]
        for head in range(HEADS_HERE):
            KM[number, head] = jnp.where(head_of == head, keys, jnp.zeros_like(keys))
            VM[number, head] = jnp.where(head_of == head, values, jnp.zeros_like(values))

    def attend(number, half):
        count = 256 * (half + 1) if number == 0 else SEQ
        rows = slice(half * 256, half * 256 + 256)
        bias = key_fill(count)
        if number == 0:
            row = half * 256 + lax.broadcasted_iota(jnp.int32, (256, count), 0)
            col = lax.broadcasted_iota(jnp.int32, (256, count), 1)
            bias = jnp.where(col <= row, bias, NEG_FILL)
        query = Q[number, rows]
        mixed = jnp.zeros((256, COLS), F32)
        for head in range(HEADS_HERE):
            scores = nt(query, KM[number, head, :count]) + bias
            expo = jnp.exp(scores - jnp.max(scores, -1, keepdims=True))
            prob = (expo * (1.0 / jnp.sum(expo, -1, keepdims=True))).astype(BF)
            PR[number, head, rows, :count] = prob
            mixed = mixed + nn(prob, VM[number, head, :count])
        A[number, rows] = mixed.astype(BF)

    def attend_back(number, half):
        count = 256 * (half + 1) if number == 0 else SEQ
        rows = slice(half * 256, half * 256 + 256)
        grad_o = DO[rows]
        grad_q = jnp.zeros((256, COLS), F32)
        for head in range(HEADS_HERE):
            grad_p = nt(grad_o, VM[number, head, :count])
            prob = PR[number, head, rows, :count].astype(F32)
            inner = jnp.sum(prob * grad_p, -1, keepdims=True)
            grad_s = (prob * (grad_p - inner)).astype(BF)
            DS[head, rows, :count] = grad_s
            grad_q = grad_q + nn(grad_s, KM[number, head, :count])
        DQ[rows] = (grad_q * HD**-0.5).astype(BF)

    def turned_product(number, table, source, target):
        source_t = source[...].T
        for head in range(HEADS_HERE):
            part = slice(head * HD, (head + 1) * HD)
            if number == 0:
                TR[part, 0:256] = nn(source_t[part], table[head, :, 0:256]).astype(BF)
                TR[part, 256:512] = nn(
                    source_t[part, 256:512], table[head, 256:512, 256:512]
                ).astype(BF)
            else:
                TR[part] = nn(source_t[part], table[head]).astype(BF)
        target[...] = TR[...].T

    def value_back(number):
        turned_product(number, PR.at[number], DO, DV)

    def key_back(number):
        turned_product(number, DS, Q.at[number], DK)

    def norms_pass():
        for copy in nb_first:
            copy.wait_recv()
        nb_second.append(send(NB.at[:, y], NB.at[:, y], nb_s.at[nz - 1], nb_r.at[nz - 1], y_peer))

    def gains():
        nb_second[0].wait_recv()
        per_column = nz // 4
        for column in range(4):
            first = column * per_column
            total = NB[first, 0] + NB[first, 1]
            for at in range(first + 1, first + per_column):
                total = total + NB[at, 0] + NB[at, 1]
            GAIN[:, column * 128 : (column + 1) * 128] = total
        NGR[...] = jnp.zeros_like(NGR)

    def fetched():
        for fetch in fetches[5:]:
            fetch.wait()

    def first_norm():
        each_rows(lambda rows, first: norm_rows(0, rows, tok[rows].astype(F32)))

    def cotangent_rows():
        def dead_rows(rows, first):
            places = first + lax.broadcasted_iota(jnp.int32, (128, 1), 0)
            DZ[rows] = jnp.where(live_of(places), cot[rows].astype(F32), 0.0).astype(BF)

        each_rows(dead_rows)
        HT[4] = DZ[...].T

    def memory_turned():
        HT[1] = mem[...].T

    def self_queries():
        Q[0] = (nn(H[0], weight(WQ1)) * HD**-0.5).astype(BF)
        K[0] = nn(H[0], weight(WK1)).astype(BF)

    def self_values():
        V[0] = nn(H[0], weight(WV1)).astype(BF)
        split_heads(0)

    def project(number):
        out_w = weight(WO2 if number else WO1)
        swap_rows(number, lambda rows: nt(A[number, rows], out_w))

    def memory_keys():
        K[1] = nn(mem[...], weight(WK2)).astype(BF)
        V[1] = nn(mem[...], weight(WV2)).astype(BF)
        split_heads(1)

    def second_norm():
        def second_rows(rows, first):
            values = tok[rows].astype(F32) + swap_sum(0, rows)
            XF[rows] = values
            norm_rows(1, rows, values)

        each_rows(second_rows, 0)

    def cross_queries():
        Q[1] = (nn(H[1], weight(WQ2)) * HD**-0.5).astype(BF)

    def turn(number):
        HT[number + 1 if number else 0] = H[number].T

    def third_norm():
        def third_rows(rows, first):
            values = XF[rows] + swap_sum(1, rows)
            XF[rows] = values
            norm_rows(2, rows, values)

        each_rows(third_rows, 1)

    def hidden_chunk(chunk):
        up, down = weight(8 + 2 * chunk), weight(9 + 2 * chunk)

        def hidden_rows(rows, first):
            hidden = nn(H[2, rows], up)
            grad_act = nn(DZ[rows], down)
            gate = 0.5 + 0.5 * lax.erf(hidden * 0.5**0.5)
            slope = gate + hidden * jnp.exp(-0.5 * hidden * hidden) * 0.3989422804014327
            act = (hidden * gate).astype(BF)
            grad_u = (grad_act * slope).astype(BF)
            ACT[rows] = act
            DU[rows] = grad_u
            if chunk == 0:
                OACC[rows] = nt(act, down)
                DHA[rows] = nt(grad_u, up)
            else:
                OACC[rows] += nt(act, down)
                DHA[rows] += nt(grad_u, up)

        for half in range(2):
            hidden_rows(slice(half * 256, half * 256 + 256), half * 256)

    def hidden_grads(chunk):
        put_grad(8 + 2 * chunk, nn(HT[3], DU[...]))
        put_grad(9 + 2 * chunk, nn(HT[4], ACT[...]))

    def hidden_swap():
        swap_rows(3, lambda rows: DHA[rows])

    def out_swap():
        swap_rows(2, lambda rows: OACC[rows])

    def back_third():
        def one(rows, first):
            grad = DZ[rows].astype(F32) + norm_back(2, rows, swap_sum(3, rows))
            DX[rows] = grad
            H[2, rows] = grad.astype(BF)

        each_rows(one, 3)

    def back_second():
        def one(rows, first):
            grad = DX[rows] + norm_back(1, rows, swap_sum(4, rows))
            DX[rows] = grad
            H[2, rows] = grad.astype(BF)

        each_rows(one, 4)

    def back_first():
        def one(rows, first):
            grad = DX[rows] + norm_back(0, rows, swap_sum(5, rows))
            tgrad[x, rows] = grad.astype(BF)

        each_rows(one, 5)

    def project_back(number):
        block = WO2 if number else WO1
        DO[...] = nn(H[2], weight(block)).astype(BF)
        put_grad(block, nn(H[2].T, A[number]))

    def cross_query_back():
        up = weight(WQ2)
        swap_rows(4, lambda rows: nt(DQ[rows], up))

    def weight_grad(block, turned, grads):
        put_grad(block, nn(HT[turned], (DQ, DK, DV)[grads][...]))

    def self_back():
        w_q, w_k, w_v = weight(WQ1), weight(WK1), weight(WV1)
        swap_rows(5, lambda rows: nt(DQ[rows], w_q) + nt(DK[rows], w_k) + nt(DV[rows], w_v))

    half_own = pl.ds(pl.multiple_of(core * 256, 256), 256)
    shares = {}

    def share_start(number):
        part = (bout, tgrad)[number].at[x, half_own]
        shares[number, 0] = send(part, part, out_s.at[number, 0], out_r.at[number, 0], x_peer)

    def share_pass(number):
        shares[number, 0].wait_recv()
        part = (bout, tgrad)[number].at[1 - x, half_own]
        shares[number, 1] = send(part, part, out_s.at[number, 1], out_r.at[number, 1], sibling)

    def share_done(number):
        shares[number, 1].wait_recv()
        store((bout, tgrad)[number], (bout_hbm, tgrad_hbm)[number])

    def out_rows():
        def one(rows, first):
            bout[x, rows] = (XF[rows] + swap_sum(2, rows)).astype(BF)

        each_rows(one, 2)

    norm_sends = {}

    def norm_grads_start():
        for row in range(6):
            NX[0, row : row + 1] = jnp.sum(NGR[row], 0, keepdims=True)
        NX[0, 6:8] = jnp.zeros((2, WIDTH), F32)
        norm_sends["x"] = send(NX.at[0], NX.at[1], ng_s.at[0], ng_r.at[0], x_peer)

    def norm_grads_mid():
        norm_sends["x"].wait_recv()
        NY[0] = NX[0] + NX[1]
        norm_sends["y"] = send(NY.at[0], NY.at[1], ng_s.at[1], ng_r.at[1], y_peer)

    def norm_grads_last():
        norm_sends["y"].wait_recv()
        NZB[nz - 1] = NY[0] + NY[1]
        norm_sends["z"] = [
            send(NZB.at[nz - 1], NZB.at[s - 1], ng_s.at[1 + s], ng_r.at[1 + s], z_peer[s])
            for s in range(1, nz)
        ]

    def norm_grads_done():
        total = NZB[nz - 1]
        for s in range(1, nz):
            norm_sends["z"][s - 1].wait_recv()
            total = total + NZB[s - 1]
        NT[...] = total
        column = pl.ds(pl.multiple_of(dp * rows_own // 128 * 128, 128), 128)
        nsum[...] = pltpu.roll(NT[:, column], lax.rem(128 - lane_at, 128), 1)

    stored = []

    def store(src, dst):
        copy = pltpu.make_async_copy(src, dst, lsem.at[8 + len(stored)])
        copy.start()
        stored.append(copy)

    def finish():
        store(gsum, gsum_hbm)
        store(nsum, nsum_hbm)
        for copy in pending:
            copy.wait_send()
        for copy in stored:
            copy.wait()

    plan = (
        (gather, 1, 0), (gather, 14, 0), (gather, 0, 0), (gather, 15, 0), (gather, 2, 0), (fetched,),
        (cotangent_rows,), (gather, 5, 0), (memory_turned,), (gather, 3, 0), (gather, 4, 0), (gather, 14, 1),
        (norms_pass,), (gather, 15, 1), (gather, 1, 1), (gather, 6, 0), (gather, 0, 1), (gather, 7, 0),
        (gather, 2, 1), (gather, 8, 0), (gains,), (first_norm,), (gather, 5, 1), (turn, 0), (gather, 10, 0),
        (gather, 1, 2), (gather, 3, 1), (gather, 9, 0), (gather, 0, 2), (gather, 4, 1), (gather, 11, 0),
        (gather, 2, 2), (gather, 6, 1), (gather, 13, 0), (gather, 5, 2), (gather, 7, 1), (gather, 12, 0),
        (gather, 3, 2), (gather, 14, 2), (gather, 1, 3), (gather, 0, 3), (self_queries,), (gather, 8, 1),
        (gather, 4, 2), (gather, 9, 1), (gather, 10, 1), (gather, 6, 2), (gather, 2, 3), (self_values,),
        (attend, 0, 0), (gather, 15, 2), (gather, 5, 3), (attend, 0, 1), (gather, 11, 1), (gather, 7, 2),
        (gather, 12, 1), (gather, 13, 1), (gather, 3, 3), (project, 0), (gather, 4, 3), (memory_keys,),
        (gather, 8, 2), (second_norm,), (gather, 9, 2), (turn, 1), (gather, 14, 3), (gather, 10, 2),
        (gather, 6, 3), (cross_queries,), (attend, 1, 1), (gather, 7, 3), (gather, 11, 2), (attend, 1, 0),
        (gather, 13, 2), (gather, 12, 2), (project, 1), (gather, 15, 3), (gather, 9, 3), (gather, 8, 3),
        (third_norm,), (hidden_chunk, 0), (turn, 2), (hidden_grads, 0), (total, 0, 0), (total, 1, 0),
        (gather, 10, 3), (gather, 11, 3), (hidden_chunk, 1), (hidden_grads, 1), (total, 3, 0), (total, 2, 0),
        (gather, 13, 3), (gather, 12, 3), (hidden_chunk, 2), (hidden_grads, 2), (total, 4, 0),
        (hidden_chunk, 3), (out_swap,), (hidden_swap,), (total, 0, 1), (hidden_grads, 3), (total, 6, 0),
        (total, 7, 0), (total, 5, 0), (out_rows,), (share_start, 0), (back_third,), (project_back, 1),
        (attend_back, 1, 0), (total, 3, 1), (value_back, 1), (total, 4, 1), (total, 8, 0),
        (attend_back, 1, 1), (weight_grad, WQ2, 2, 0), (total, 10, 0), (cross_query_back,),
        (weight_grad, WV2, 1, 2), (key_back, 1), (total, 9, 0), (total, 5, 1), (back_second,),
        (project_back, 0), (attend_back, 0, 0), (total, 6, 1), (total, 7, 1), (total, 1, 1), (total, 2, 1),
        (total, 12, 0), (attend_back, 0, 1), (total, 10, 1), (total, 4, 2), (share_pass, 0), (total, 0, 2),
        (weight_grad, WQ1, 0, 0), (total, 14, 0), (weight_grad, WK2, 1, 1), (total, 11, 0), (key_back, 0),
        (total, 3, 2), (weight_grad, WK1, 0, 1), (share_done, 0), (value_back, 0), (total, 9, 1),
        (total, 8, 1), (total, 15, 0), (total, 2, 2), (total, 1, 2), (total, 5, 2), (weight_grad, WV1, 0, 2),
        (total, 13, 0), (self_back,), (total, 10, 2), (total, 12, 1), (total, 4, 3), (total, 0, 3),
        (back_first,), (total, 11, 1), (total, 14, 1), (norm_grads_start,), (share_start, 1), (total, 8, 2),
        (total, 3, 3), (total, 1, 3), (total, 2, 3), (total, 9, 2), (total, 5, 3), (total, 15, 1),
        (total, 13, 1), (total, 10, 3), (norm_grads_mid,), (total, 6, 2), (total, 7, 2), (total, 8, 3),
        (total, 12, 2), (total, 11, 2), (total, 14, 2), (total, 9, 3), (norm_grads_last,), (total, 15, 2),
        (share_pass, 1), (total, 6, 3), (total, 7, 3), (total, 13, 2), (total, 11, 3), (share_done, 1),
        (total, 12, 3), (total, 14, 3), (norm_grads_done,), (total, 15, 3), (total, 13, 3), (finish,),
    )
    for step, *of in plan:
        step(*of)


def update(weight, grad, moment, average, rate):
    moment_new = MOMENTUM * moment + grad
    weight_new = weight - rate * (grad + MOMENTUM * moment_new)
    average_new = AVG_DECAY * average + (1.0 - AVG_DECAY) * weight_new
    return moment_new, weight_new, average_new


def update_kernel(rate_scale, gsum_hbm, nsum_hbm, tlow_hbm, bout_hbm, *refs):
    sources, targets = refs[0:15], refs[15:37]
    gsum, nsum, tlow, bout, tgrad, *held, in_sems, out_sems = refs[37:]
    fetched, results = held[0:15], held[15:35]
    moves = (
        (tlow_hbm, tlow), (bout_hbm, bout), (gsum_hbm, gsum), (nsum_hbm, nsum),
        *zip(sources, fetched),
    )
    fetches = [
        pltpu.make_async_copy(src, dst, in_sems.at[number])
        for number, (src, dst) in enumerate(moves)
    ]
    for fetch in fetches:
        fetch.start()
    stores = []

    def store(src, number):
        copy = pltpu.make_async_copy(src, targets[number], out_sems.at[number])
        copy.start()
        stores.append(copy)

    fetches[0].wait()
    tgrad[...] = tlow[...].astype(F32)
    store(tgrad, 1)
    fetches[1].wait()
    store(bout, 0)
    fetches[2].wait()
    fetches[3].wait()
    for which in range(5):
        weight, moment, average = fetched[which], fetched[5 + which], fetched[10 + which]
        for turn in range(3):
            fetches[4 + 5 * turn + which].wait()
        if which < 4:
            parts = [
                ((index,) if which < 2 else (slice(None), slice(index * 128, index * 128 + 128)), gsum[block])
                for block, (array, index) in enumerate(BLOCK_OF)
                if array == which
            ]
        else:
            parts = [((slice(None), slice(None)), nsum[0:6, 0 : weight.shape[1]])]
        for at, grad in parts:
            rate = BASE_RATES[which] * rate_scale
            found = update(weight[at], grad, moment[at], average[at], rate)
            for number, value in enumerate((grad, *found)):
                results[4 * which + number][at] = value
        for number in range(4):
            store(results[4 * which + number], 2 + 4 * which + number)
    for copy in stores:
        copy.wait()


def per_device(nz, *args):
    (tokens, memory, cotangent, lengths, breaks, attn_in, attn_out, ffn_in, ffn_out, norms) = args[:10]
    moments, averages = args[10:15], args[15:20]
    own = attn_in.shape[1]
    whole = (nz, 2, own, 128)
    smem = pl.BlockSpec(memory_space=pltpu.SMEM)
    hbm = pl.BlockSpec(memory_space=pl.ANY)
    dma = pltpu.SemaphoreType.DMA

    def bf(*shape):
        return pltpu.VMEM(shape, BF)

    def f32(*shape):
        return pltpu.VMEM(shape, F32)

    def landing(parcel, phase):
        _, count, route = parcel
        sizes = {"x": 2, "y": 2, "z": nz}
        left = [axis for axis in "xyz" if axis not in route[: phase + 1]]
        senders = nz - 1 if route[phase] == "z" else 1
        sides = [2] if "x" in left else []
        rest = [sizes[axis] for axis in "zy" if axis in left]
        return bf(senders, *sides, count, *rest, own, 128)

    landings = [[landing(parcel, phase) for phase in range(3)] for parcel in SUM]
    scratch = [
        f32(BLOCKS, own, 128), f32(8, 128), bf(2, SEQ, WIDTH), bf(2, SEQ, WIDTH),
        *[f32(*array.shape) for array in (attn_in, attn_out, ffn_in, ffn_out, norms)],
        bf(SEQ, WIDTH), bf(SEQ, WIDTH), bf(SEQ, WIDTH),
        bf(2, BLOCKS, *whole), bf(2, BLOCKS, *whole),
        landings,
        f32(nz, 2, 8, 128), f32(8, 128), f32(8, WIDTH),
        f32(6, 8, WIDTH), f32(2, 8, WIDTH), f32(2, 8, WIDTH), f32(nz, 8, WIDTH),
        f32(8, WIDTH),
        bf(6, SEQ, WIDTH), bf(6, SEQ, WIDTH),
        f32(SEQ, WIDTH), f32(3, SEQ, WIDTH), f32(3, SEQ, 1),
        f32(SEQ, WIDTH), f32(SEQ, WIDTH),
        bf(3, SEQ, WIDTH), bf(5, WIDTH, SEQ),
        bf(2, SEQ, COLS), bf(2, SEQ, COLS), bf(2, SEQ, COLS),
        bf(2, HEADS_HERE, SEQ, COLS), bf(2, HEADS_HERE, SEQ, COLS),
        bf(2, HEADS_HERE, SEQ, SEQ), bf(HEADS_HERE, SEQ, SEQ),
        bf(2, SEQ, COLS), f32(SEQ, WIDTH),
        bf(SEQ, COLS), bf(SEQ, COLS), bf(SEQ, COLS),
        bf(SEQ, COLS), bf(SEQ, COLS), bf(SEQ, WIDTH), bf(SEQ, COLS), bf(COLS, SEQ),
        dma((12,)), dma((len(GATHER),)), dma((len(GATHER), 3)),
        dma((len(SUM),)), dma((len(SUM), 3)),
        dma((nz,)), dma((nz,)),
        dma((6, 2)), dma((6, 2)),
        dma((nz + 1,)), dma((nz + 1,)), dma((2, 2)), dma((2, 2)),
    ]
    gsum, nsum, bout, tlow = pl.pallas_call(
        functools.partial(layer_kernel, nz),
        out_shape=(
            jax.ShapeDtypeStruct((BLOCKS, own, 128), F32),
            jax.ShapeDtypeStruct((8, 128), F32),
            jax.ShapeDtypeStruct((2, SEQ, WIDTH), BF),
            jax.ShapeDtypeStruct((2, SEQ, WIDTH), BF),
        ),
        in_specs=[hbm] * 3 + [smem] * 2 + [hbm] * 5,
        out_specs=(hbm,) * 4,
        scratch_shapes=scratch,
        compiler_params=pltpu.CompilerParams(
            collective_id=0, has_side_effects=True, vmem_limit_bytes=58 * 2**20
        ),
    )(tokens, memory, cotangent, lengths, breaks, attn_in, attn_out, ffn_in, ffn_out, norms)
    weights = (attn_in, attn_out, ffn_in, ffn_out, norms)
    rate_scale = float(lax.axis_size("dp") * tokens.shape[0]) ** -0.5
    results = pl.pallas_call(
        functools.partial(update_kernel, rate_scale),
        out_shape=(
            jax.ShapeDtypeStruct((2, SEQ, WIDTH), BF),
            jax.ShapeDtypeStruct((2, SEQ, WIDTH), F32),
            *[jax.ShapeDtypeStruct(w.shape, F32) for w in weights for _ in range(4)],
        ),
        in_specs=[hbm] * 19,
        out_specs=(hbm,) * 22,
        scratch_shapes=[
            f32(BLOCKS, own, 128), f32(8, 128), bf(2, SEQ, WIDTH), bf(2, SEQ, WIDTH), f32(2, SEQ, WIDTH),
            *[f32(*w.shape) for w in (*weights, *moments, *averages)],
            *[f32(*w.shape) for w in weights for _ in range(4)],
            dma((19,)), dma((22,)),
        ],
        compiler_params=pltpu.CompilerParams(vmem_limit_bytes=63 * 2**20),
    )(gsum, nsum, tlow, bout, *weights, *moments, *averages)
    return (results[0].reshape(tokens.shape), results[1].reshape(tokens.shape), *results[2:])


def solution(mesh):
    rows, attn, ffn, norm = P("dp", None), P(None, "dp", "tensor"), P("dp", "tensor"), P(None, "dp")
    weights = (attn, attn, ffn, ffn, norm)
    return jax.shard_map(
        functools.partial(per_device, mesh.shape["dp"] // 2),
        mesh=mesh,
        in_specs=(rows, rows, rows, P("dp"), P("dp")) + weights * 3,
        out_specs=(rows, rows) + tuple(spec for spec in weights for _ in range(4)),
        check_vma=False,
    )
```

```python
import functools

import jax
import jax.numpy as jnp
from jax import lax
from jax.experimental import pallas as pl
from jax.experimental.pallas import tpu as pltpu
from jax.sharding import PartitionSpec as P

HD = 64
SEQ = 512
WIDTH = 512
LINKER = 10
EPSILON = 1e-05
NEG_FILL = -1000000000.0
MOMENTUM = 0.9
AVG_DECAY = 0.6
BASE_RATES = (0.05, 1.0, 0.05, 0.05, 0.3)

BF = jnp.bfloat16
F32 = jnp.float32
MESH = pl.DeviceIdType.MESH
HEADS_HERE = 4
COLS = 256
BLOCKS = 16
BLOCK_OF = (
    (0, 0), (0, 1), (0, 2), (1, 0),
    (0, 4), (0, 5), (0, 3), (1, 1),
    (2, 0), (3, 0), (2, 1), (3, 1),
    (2, 2), (3, 2), (2, 3), (3, 3),
)
WQ1, WK1, WV1, WO1, WK2, WV2, WQ2, WO2 = range(8)
GATHER = (
    (0, 1, "zyx"), (1, 1, "zxy"), (2, 1, "zyx"), (3, 1, "yxz"),
    (4, 1, "zyx"), (5, 1, "zxy"), (6, 1, "zyx"), (7, 1, "yxz"),
    (8, 1, "zyx"), (9, 1, "zxy"), (10, 1, "zyx"), (11, 1, "zxy"),
    (12, 1, "xyz"), (13, 1, "zyx"), (14, 1, "xyz"), (15, 1, "xyz"),
)
SUM = (
    (8, 1, "xzy"), (9, 1, "zyx"), (10, 1, "xyz"), (11, 1, "yxz"),
    (12, 1, "yxz"), (13, 1, "yzx"), (14, 1, "yxz"), (15, 1, "zyx"),
    (7, 1, "zyx"), (5, 1, "yzx"), (6, 1, "yxz"), (4, 1, "xyz"),
    (3, 1, "yxz"), (2, 1, "yxz"), (0, 1, "xyz"), (1, 1, "yxz"),
)


def nn(left, right):
    return jnp.dot(left, right, preferred_element_type=F32)


def nt(left, right):
    return lax.dot_general(left, right, (((1,), (1,)), ((), ())), preferred_element_type=F32)


class Flight:
    def __init__(self, wait_recv, wait_send, relay):
        self.wait_recv, self.wait_send, self.relay = wait_recv, wait_send, relay


def layer_kernel(
    nz,
    tok_hbm, mem_hbm, cot_hbm, len_ref, brk_ref, ain_hbm, aout_hbm, fin_hbm, fout_hbm, norms_hbm,
    gsum_hbm, nsum_hbm, bout_hbm, tgrad_hbm,
    gsum, nsum, bout, tgrad, ain, aout, fin, fout, norms, tok, mem, cot, W, G, R, NB, NP, GAIN, NGR, NX, NY, NZB, NT,
    XS, XR, XF, XH, IV, OACC, DHA, H, HT, Q, K, V, KM, VM, PR, DS, A, DX, DQ, DK, DV,
    ACT, DU, DZ, DO, TR,
    lsem, ag_s, ag_r, ag_f, rs_s, rs_r, nb_s, nb_r, xc_s, xc_r,
    ng_s, ng_r, out_s, out_r,
):
    dp, tensor = lax.axis_index("dp"), lax.axis_index("tensor")
    z, y, x, core = dp // 2, dp % 2, tensor // 2, tensor % 2
    rows_own = ain.shape[1]
    sibling = (dp, x * 2 + 1 - core)
    x_peer = (dp, (1 - x) * 2 + core)
    y_peer = (z * 2 + 1 - y, tensor)
    z_of = [None] + [lax.rem(z + step, nz) for step in range(1, nz)]
    z_peer = [None] + [(z_of[step] * 2 + y, tensor) for step in range(1, nz)]
    pending = []

    def send(src, dst, send_sem, recv_sem, peer, alone=True):
        copy = pltpu.make_async_remote_copy(
            src, dst, send_sem, recv_sem, device_id=peer, device_id_type=MESH
        )
        copy.start()
        if alone:
            pending.append(copy)
        return copy

    barrier = pltpu.get_barrier_semaphore()
    peers = [sibling, x_peer, y_peer] + z_peer[1:]
    for peer in peers:
        pl.semaphore_signal(barrier, inc=1, device_id=peer, device_id_type=MESH)
    mine = pl.ds(pl.multiple_of(x * SEQ, SEQ), SEQ)
    moves = (
        (norms_hbm, norms), (ain_hbm, ain), (aout_hbm, aout), (fin_hbm, fin), (fout_hbm, fout),
        (tok_hbm.at[mine], tok), (mem_hbm.at[mine], mem), (cot_hbm.at[mine], cot),
    )
    fetches = []
    for number, (src, dst) in enumerate(moves):
        fetch = pltpu.make_async_copy(src, dst, lsem.at[number])
        fetch.start()
        fetches.append(fetch)
    for fetch in fetches[:5]:
        fetch.wait()

    NP[...] = jnp.zeros_like(NP)
    NP[0:6, 0:rows_own] = norms[...].astype(BF).astype(F32)
    lane_at = lax.rem(dp * rows_own, 128)
    NB[z, y] = pltpu.roll(NP[...], lane_at, 1)

    def own_block(arrays, block):
        array, index = BLOCK_OF[block]
        if array < 2:
            return arrays[array][index]
        return arrays[array][:, index * 128 : (index + 1) * 128]

    for block in range(BLOCKS):
        W[x, block, z, y] = own_block((ain, aout, fin, fout), block).astype(BF)
    pl.semaphore_wait(barrier, len(peers))

    me_of = {"x": x, "y": y, "z": z}
    flights, nb_second = {}, []

    def send_all(key, axis, pieces, whole, sems):
        if axis == "z":
            copies = [(z_of[s], s - 1, z_peer[s]) for s in range(1, nz)]
        elif axis == "y":
            copies = [(1 - y, 0, y_peer)]
        else:
            copies = [(1 - x, 0, x_peer)]
        for place, slot, peer in copies:
            send(*pieces(place, slot), *sems, peer, False)
        flights[key] = pltpu.make_async_remote_copy(
            *whole, *sems, device_id=copies[0][2], device_id_type=MESH
        )
        if key[2] == 2:
            pending.append(flights[key])

    def landed(key):
        flights[key].wait_recv()
        if key[2] < 2:
            flights[key].wait_send()

    def place_of(done, blocks):
        at = {axis: slice(None) if axis in done else me_of[axis] for axis in "xyz"}
        return at, lambda: (at["x"], blocks, at["z"], at["y"])

    far = lax.rem(z + 2, nz)
    in_middle = (z == 1) | (z == 2)

    def z_gather(parcel, part, at, where):
        sems = (ag_s.at[parcel], ag_r.at[parcel, GATHER[parcel][2].index("z")])

        def copy_to(src, place, send_sem, recv_sem):
            return pltpu.make_async_remote_copy(
                src, src, send_sem, recv_sem, device_id=(place * 2 + y, tensor), device_id_type=MESH
            )

        def of(count):
            at["z"] = pl.ds(0, count)
            return W.at[where()]

        copy_to(part, z_of[2], sems[0], ag_f.at[parcel]).start()
        for s, end in ((1, 3), (3, 0)):

            @pl.when(z != end)
            def _(s=s):
                copy_to(part, z_of[s], *sems).start()

        at["z"] = far
        on = copy_to(W.at[where()], 3 - far, *sems)

        def relay():
            copy_to(of(1), z_of[2], sems[0], ag_f.at[parcel]).wait_recv()

            @pl.when(in_middle)
            def _():
                copy_to(of(3), z_of[2], *sems).wait_send()
                on.start()

        def wait_recv():
            copy_to(of(2), z_of[2], *sems).wait_recv()

        def wait_send():
            @pl.when(in_middle)
            def _():
                on.wait_send()

            @pl.when(jnp.logical_not(in_middle))
            def _():
                copy_to(of(2), z_of[2], *sems).wait_send()

        return Flight(wait_recv, wait_send, relay)

    def gather(parcel, phase):
        if phase > 0:
            landed(("gather", parcel, phase - 1))
        if phase == 3:
            return
        first, count, route = GATHER[parcel]
        at, where = place_of(route[:phase], pl.ds(first, count))
        part = W.at[where()]
        sems = (ag_s.at[parcel], ag_r.at[parcel, phase])
        key = ("gather", parcel, phase)
        if route[phase] == "z" and nz == 4:
            flights[key] = z_gather(parcel, part, at, where)
            if phase == 2:
                pending.append(flights[key])
            return
        if route[phase] == "z":
            at["z"] = pl.ds(0, nz - 1)
        much = W.at[where()]
        send_all(key, route[phase], lambda place, slot: (part, part), (much, much), sems)

    def relay(parcel):
        if nz == 4:
            flights["gather", parcel, GATHER[parcel][2].index("z")].relay()

    nb_first = [
        send(NB.at[z, y], NB.at[z, y], nb_s.at[s - 1], nb_r.at[s - 1], z_peer[s])
        for s in range(1, nz)
    ]

    def weight(block):
        return jnp.concatenate(
            [W[0, block].reshape(WIDTH, 128), W[1, block].reshape(WIDTH, 128)], axis=1
        )

    def put_grad(block, value):
        low = value.astype(BF)
        G[0, block] = low[:, :128].reshape(G.shape[2:])
        G[1, block] = low[:, 128:].reshape(G.shape[2:])

    def total(parcel, phase):
        first, count, route = SUM[parcel]
        if phase > 0:
            landed(("sum", parcel, phase - 1))
            into = R[parcel][phase - 1]
            left = [axis for axis in "xyz" if axis not in route[:phase]]
            at, _ = place_of([axis for axis in left], None)
            for number in range(count):
                for side in range(2) if "x" in left else (x,):
                    here = (side, first + number, at["z"], at["y"])
                    found = G[here].astype(F32)
                    for slot in range(nz - 1 if route[phase - 1] == "z" else 1):
                        landing = into[slot, side, number] if "x" in left else into[slot, number]
                        found = found + landing.astype(F32)
                    if phase == 3:
                        gsum[first + number] = found
                    else:
                        G[here] = found.astype(BF)
        if phase == 3:
            return
        axis, into = route[phase], R[parcel][phase]
        at, where = place_of([a for a in "xyz" if a not in route[:phase]], pl.ds(first, count))

        def pieces(place, slot):
            at[axis] = place
            return G.at[where()], into.at[slot]

        at[axis] = pl.ds(0, nz - 1) if axis == "z" else me_of[axis]
        much = G.at[where()]
        sems = (rs_s.at[parcel], rs_r.at[parcel, phase])
        send_all(("sum", parcel, phase), axis, pieces, (much, into if axis == "z" else into.at[0]), sems)

    xc = {}

    def swap_start(number, half):
        rows = pl.ds(half * 256, 256)
        xc[number, half] = send(
            XS.at[number, rows],
            XR.at[number, rows],
            xc_s.at[number, half],
            xc_r.at[number, half],
            sibling,
        )

    def swap_sum(number, rows):
        return XS[number, rows].astype(F32) + XR[number, rows].astype(F32)

    def swap_rows(number, make):
        for half in range(2):
            rows = slice(half * 256, half * 256 + 256)
            XS[number, rows] = make(rows).astype(BF)
            swap_start(number, half)

    def each_rows(body, swap=None):
        for first in range(0, SEQ, 128):
            if swap is not None and first % 256 == 0:
                xc[swap, first // 256].wait_recv()
            body(slice(first, first + 128), first)

    def norm_rows(number, rows, values):
        center = values - jnp.mean(values, -1, keepdims=True)
        inv_std = lax.rsqrt(jnp.mean(center * center, -1, keepdims=True) + EPSILON)
        x_hat = center * inv_std
        XH[number, rows] = x_hat
        IV[number, rows] = inv_std
        gain, bias = GAIN[2 * number : 2 * number + 1], GAIN[2 * number + 1 : 2 * number + 2]
        H[number, rows] = (x_hat * gain + bias).astype(BF)

    def norm_back(number, rows, grad_h):
        x_hat, inv_std = XH[number, rows], IV[number, rows]
        NGR[2 * number] += jnp.sum((grad_h * x_hat).reshape(-1, 8, WIDTH), 0)
        NGR[2 * number + 1] += jnp.sum(grad_h.reshape(-1, 8, WIDTH), 0)
        grad_hat = grad_h * GAIN[2 * number : 2 * number + 1]
        return inv_std * (
            grad_hat
            - jnp.mean(grad_hat, -1, keepdims=True)
            - x_hat * jnp.mean(grad_hat * x_hat, -1, keepdims=True)
        )

    length_n, break_n = len_ref[x], brk_ref[x]

    def live_of(places):
        linker = (places >= break_n) & (places < break_n + LINKER)
        return (places < length_n) & jnp.logical_not(linker)

    def key_fill(count):
        places = lax.broadcasted_iota(jnp.int32, (1, count), 1)
        return jnp.where(live_of(places), 0.0, NEG_FILL)

    head_of = lax.broadcasted_iota(jnp.int32, (1, COLS), 1) // HD

    def split_heads(number):
        keys, values = K[number], V[number]
        for head in range(HEADS_HERE):
            KM[number, head] = jnp.where(head_of == head, keys, jnp.zeros_like(keys))
            VM[number, head] = jnp.where(head_of == head, values, jnp.zeros_like(values))

    def attend(number, half):
        count = 256 * (half + 1) if number == 0 else SEQ
        rows = slice(half * 256, half * 256 + 256)
        bias = key_fill(count)
        if number == 0:
            row = half * 256 + lax.broadcasted_iota(jnp.int32, (256, count), 0)
            col = lax.broadcasted_iota(jnp.int32, (256, count), 1)
            bias = jnp.where(col <= row, bias, NEG_FILL)
        query = Q[number, rows]
        mixed = jnp.zeros((256, COLS), F32)
        for head in range(HEADS_HERE):
            scores = nt(query, KM[number, head, :count]) + bias
            expo = jnp.exp(scores - jnp.max(scores, -1, keepdims=True))
            prob = (expo * (1.0 / jnp.sum(expo, -1, keepdims=True))).astype(BF)
            PR[number, head, rows, :count] = prob
            mixed = mixed + nn(prob, VM[number, head, :count])
        A[number, rows] = mixed.astype(BF)

    def attend_back(number, half):
        count = 256 * (half + 1) if number == 0 else SEQ
        rows = slice(half * 256, half * 256 + 256)
        grad_o = DO[rows]
        grad_q = jnp.zeros((256, COLS), F32)
        for head in range(HEADS_HERE):
            grad_p = nt(grad_o, VM[number, head, :count])
            prob = PR[number, head, rows, :count].astype(F32)
            inner = jnp.sum(prob * grad_p, -1, keepdims=True)
            grad_s = (prob * (grad_p - inner)).astype(BF)
            DS[head, rows, :count] = grad_s
            grad_q = grad_q + nn(grad_s, KM[number, head, :count])
        DQ[rows] = (grad_q * HD**-0.5).astype(BF)

    def turned_product(number, table, source, target):
        source_t = source[...].T
        for head in range(HEADS_HERE):
            part = slice(head * HD, (head + 1) * HD)
            if number == 0:
                TR[part, 0:256] = nn(source_t[part], table[head, :, 0:256]).astype(BF)
                TR[part, 256:512] = nn(
                    source_t[part, 256:512], table[head, 256:512, 256:512]
                ).astype(BF)
            else:
                TR[part] = nn(source_t[part], table[head]).astype(BF)
        target[...] = TR[...].T

    def value_back(number):
        turned_product(number, PR.at[number], DO, DV)

    def key_back(number):
        turned_product(number, DS, Q.at[number], DK)

    def norms_pass():
        for copy in nb_first:
            copy.wait_recv()
        nb_second.append(send(NB.at[:, y], NB.at[:, y], nb_s.at[nz - 1], nb_r.at[nz - 1], y_peer))

    def gains():
        nb_second[0].wait_recv()
        per_column = nz // 4
        for column in range(4):
            first = column * per_column
            total = NB[first, 0] + NB[first, 1]
            for at in range(first + 1, first + per_column):
                total = total + NB[at, 0] + NB[at, 1]
            GAIN[:, column * 128 : (column + 1) * 128] = total
        NGR[...] = jnp.zeros_like(NGR)

    def fetched():
        for fetch in fetches[5:]:
            fetch.wait()

    def first_norm():
        each_rows(lambda rows, first: norm_rows(0, rows, tok[rows].astype(F32)))

    def cotangent_rows():
        def dead_rows(rows, first):
            places = first + lax.broadcasted_iota(jnp.int32, (128, 1), 0)
            DZ[rows] = jnp.where(live_of(places), cot[rows].astype(F32), 0.0).astype(BF)

        each_rows(dead_rows)
        HT[4] = DZ[...].T

    def memory_turned():
        HT[1] = mem[...].T

    def self_queries():
        Q[0] = (nn(H[0], weight(WQ1)) * HD**-0.5).astype(BF)
        K[0] = nn(H[0], weight(WK1)).astype(BF)

    def self_values():
        V[0] = nn(H[0], weight(WV1)).astype(BF)
        split_heads(0)

    def project(number):
        out_w = weight(WO2 if number else WO1)
        swap_rows(number, lambda rows: nt(A[number, rows], out_w))

    def memory_keys():
        K[1] = nn(mem[...], weight(WK2)).astype(BF)
        V[1] = nn(mem[...], weight(WV2)).astype(BF)
        split_heads(1)

    def second_norm():
        def second_rows(rows, first):
            values = tok[rows].astype(F32) + swap_sum(0, rows)
            XF[rows] = values
            norm_rows(1, rows, values)

        each_rows(second_rows, 0)

    def cross_queries():
        Q[1] = (nn(H[1], weight(WQ2)) * HD**-0.5).astype(BF)

    def turn(number):
        HT[number + 1 if number else 0] = H[number].T

    def third_norm():
        def third_rows(rows, first):
            values = XF[rows] + swap_sum(1, rows)
            XF[rows] = values
            norm_rows(2, rows, values)

        each_rows(third_rows, 1)

    def hidden_chunk(chunk):
        up, down = weight(8 + 2 * chunk), weight(9 + 2 * chunk)

        def hidden_rows(rows, first):
            hidden = nn(H[2, rows], up)
            grad_act = nn(DZ[rows], down)
            gate = 0.5 + 0.5 * lax.erf(hidden * 0.5**0.5)
            slope = gate + hidden * jnp.exp(-0.5 * hidden * hidden) * 0.3989422804014327
            act = (hidden * gate).astype(BF)
            grad_u = (grad_act * slope).astype(BF)
            ACT[rows] = act
            DU[rows] = grad_u
            if chunk == 0:
                OACC[rows] = nt(act, down)
                DHA[rows] = nt(grad_u, up)
            else:
                OACC[rows] += nt(act, down)
                DHA[rows] += nt(grad_u, up)

        for half in range(2):
            hidden_rows(slice(half * 256, half * 256 + 256), half * 256)

    def hidden_grads(chunk):
        put_grad(8 + 2 * chunk, nn(HT[3], DU[...]))
        put_grad(9 + 2 * chunk, nn(HT[4], ACT[...]))

    def hidden_swap():
        swap_rows(3, lambda rows: DHA[rows])

    def out_swap():
        swap_rows(2, lambda rows: OACC[rows])

    def back_third():
        def one(rows, first):
            grad = DZ[rows].astype(F32) + norm_back(2, rows, swap_sum(3, rows))
            DX[rows] = grad
            H[2, rows] = grad.astype(BF)

        each_rows(one, 3)

    def back_second():
        def one(rows, first):
            grad = DX[rows] + norm_back(1, rows, swap_sum(4, rows))
            DX[rows] = grad
            H[2, rows] = grad.astype(BF)

        each_rows(one, 4)

    def back_first():
        def one(rows, first):
            grad = DX[rows] + norm_back(0, rows, swap_sum(5, rows))
            tgrad[x, rows] = grad.astype(BF)

        each_rows(one, 5)

    def project_back(number):
        block = WO2 if number else WO1
        DO[...] = nn(H[2], weight(block)).astype(BF)
        put_grad(block, nn(H[2].T, A[number]))

    def cross_query_back():
        up = weight(WQ2)
        swap_rows(4, lambda rows: nt(DQ[rows], up))

    def weight_grad(block, turned, grads):
        put_grad(block, nn(HT[turned], (DQ, DK, DV)[grads][...]))

    def self_back():
        w_q, w_k, w_v = weight(WQ1), weight(WK1), weight(WV1)
        swap_rows(5, lambda rows: nt(DQ[rows], w_q) + nt(DK[rows], w_k) + nt(DV[rows], w_v))

    half_own = pl.ds(pl.multiple_of(core * 256, 256), 256)
    shares = {}

    def share_start(number):
        part = (bout, tgrad)[number].at[x, half_own]
        shares[number, 0] = send(part, part, out_s.at[number, 0], out_r.at[number, 0], x_peer)

    def share_pass(number):
        shares[number, 0].wait_recv()
        part = (bout, tgrad)[number].at[1 - x, half_own]
        shares[number, 1] = send(part, part, out_s.at[number, 1], out_r.at[number, 1], sibling)

    def share_done(number):
        shares[number, 1].wait_recv()
        store((bout, tgrad)[number], (bout_hbm, tgrad_hbm)[number])

    def out_rows():
        def one(rows, first):
            bout[x, rows] = (XF[rows] + swap_sum(2, rows)).astype(BF)

        each_rows(one, 2)

    norm_sends = {}

    def norm_grads_start():
        for row in range(6):
            NX[0, row : row + 1] = jnp.sum(NGR[row], 0, keepdims=True)
        NX[0, 6:8] = jnp.zeros((2, WIDTH), F32)
        norm_sends["x"] = send(NX.at[0], NX.at[1], ng_s.at[0], ng_r.at[0], x_peer)

    def norm_grads_mid():
        norm_sends["x"].wait_recv()
        NY[0] = NX[0] + NX[1]
        norm_sends["y"] = send(NY.at[0], NY.at[1], ng_s.at[1], ng_r.at[1], y_peer)

    def norm_grads_last():
        norm_sends["y"].wait_recv()
        NZB[nz - 1] = NY[0] + NY[1]
        norm_sends["z"] = [
            send(NZB.at[nz - 1], NZB.at[s - 1], ng_s.at[1 + s], ng_r.at[1 + s], z_peer[s])
            for s in range(1, nz)
        ]

    def norm_grads_done():
        total = NZB[nz - 1]
        for s in range(1, nz):
            norm_sends["z"][s - 1].wait_recv()
            total = total + NZB[s - 1]
        NT[...] = total
        column = pl.ds(pl.multiple_of(dp * rows_own // 128 * 128, 128), 128)
        nsum[...] = pltpu.roll(NT[:, column], lax.rem(128 - lane_at, 128), 1)

    stored = []

    def store(src, dst):
        copy = pltpu.make_async_copy(src, dst, lsem.at[8 + len(stored)])
        copy.start()
        stored.append(copy)

    def finish():
        store(gsum, gsum_hbm)
        store(nsum, nsum_hbm)
        for copy in pending:
            copy.wait_send()
        for copy in stored:
            copy.wait()

    plan = (
        (gather, 2, 0), (gather, 1, 0), (gather, 5, 0), (gather, 15, 0), (gather, 3, 0), (gather, 0, 0),
        (gather, 7, 0), (gather, 12, 0), (gather, 14, 0), (fetched,), (gather, 9, 0), (cotangent_rows,),
        (gather, 4, 0), (gather, 6, 0), (norms_pass,), (relay, 2), (memory_turned,), (gather, 15, 1),
        (gather, 3, 1), (relay, 1), (gather, 7, 1), (gather, 12, 1), (gather, 8, 0), (relay, 5),
        (gather, 14, 1), (gather, 13, 0), (relay, 0), (gains,), (relay, 9), (first_norm,), (relay, 4),
        (gather, 15, 2), (turn, 0), (relay, 6), (gather, 2, 1), (gather, 1, 1), (relay, 8), (gather, 5, 1),
        (relay, 13), (gather, 0, 1), (gather, 9, 1), (gather, 11, 0), (gather, 4, 1), (gather, 10, 0),
        (gather, 2, 2), (gather, 1, 2), (gather, 3, 2), (relay, 15), (gather, 0, 2), (gather, 6, 1),
        (relay, 11), (gather, 8, 1), (relay, 10), (gather, 4, 2), (gather, 7, 2), (gather, 13, 1),
        (gather, 2, 3), (gather, 1, 3), (gather, 5, 2), (relay, 3), (gather, 6, 2), (gather, 15, 3),
        (gather, 0, 3), (self_queries,), (self_values,), (attend, 0, 1), (gather, 11, 1), (gather, 10, 1),
        (gather, 12, 2), (attend, 0, 0), (gather, 4, 3), (gather, 9, 2), (gather, 8, 2), (relay, 7),
        (gather, 3, 3), (project, 0), (gather, 5, 3), (memory_keys,), (gather, 6, 3), (gather, 14, 2),
        (gather, 13, 2), (second_norm,), (cross_queries,), (attend, 1, 1), (relay, 12), (gather, 7, 3),
        (gather, 11, 2), (gather, 9, 3), (gather, 10, 2), (attend, 1, 0), (gather, 8, 3), (project, 1),
        (turn, 1), (relay, 14), (gather, 13, 3), (third_norm,), (gather, 12, 3), (hidden_chunk, 0),
        (gather, 11, 3), (turn, 2), (hidden_grads, 0), (total, 1, 0), (gather, 10, 3), (total, 0, 0),
        (hidden_chunk, 1), (gather, 14, 3), (hidden_grads, 1), (total, 2, 0), (total, 3, 0),
        (hidden_chunk, 2), (hidden_grads, 2), (total, 4, 0), (hidden_chunk, 3), (out_swap,), (hidden_swap,),
        (total, 0, 1), (hidden_grads, 3), (total, 6, 0), (out_rows,), (share_start, 0), (back_third,),
        (total, 7, 0), (project_back, 1), (attend_back, 1, 0), (total, 5, 0), (attend_back, 1, 1),
        (weight_grad, WQ2, 2, 0), (total, 3, 1), (total, 10, 0), (cross_query_back,), (value_back, 1),
        (total, 8, 0), (total, 4, 1), (back_second,), (weight_grad, WV2, 1, 2), (total, 6, 1), (total, 9, 0),
        (key_back, 1), (share_pass, 0), (weight_grad, WK2, 1, 1), (total, 11, 0), (project_back, 0),
        (value_back, 0), (total, 12, 0), (weight_grad, WV1, 0, 2), (attend_back, 0, 0), (share_done, 0),
        (total, 3, 2), (total, 10, 1), (attend_back, 0, 1), (total, 13, 0), (total, 4, 2),
        (weight_grad, WQ1, 0, 0), (total, 14, 0), (total, 6, 2), (key_back, 0), (self_back,), (total, 7, 1),
        (total, 5, 1), (total, 12, 1), (total, 2, 1), (weight_grad, WK1, 0, 1), (total, 3, 3), (back_first,),
        (total, 15, 0), (share_start, 1), (total, 4, 3), (total, 10, 2), (norm_grads_start,), (total, 6, 3),
        (total, 9, 1), (total, 0, 2), (total, 11, 1), (total, 14, 1), (total, 12, 2), (total, 7, 2),
        (total, 5, 2), (total, 10, 3), (total, 13, 1), (total, 8, 1), (total, 2, 2), (total, 1, 1),
        (total, 0, 3), (total, 15, 1), (total, 11, 2), (total, 9, 2), (share_pass, 1), (norm_grads_mid,),
        (total, 7, 3), (total, 5, 3), (total, 14, 2), (total, 12, 3), (total, 8, 2), (total, 13, 2),
        (share_done, 1), (total, 1, 2), (total, 2, 3), (norm_grads_last,), (total, 15, 2), (total, 9, 3),
        (total, 11, 3), (total, 8, 3), (total, 14, 3), (total, 1, 3), (total, 13, 3), (norm_grads_done,),
        (total, 15, 3), (finish,),
    )
    for step, *of in plan:
        step(*of)


def update(weight, grad, moment, average, rate):
    moment_new = MOMENTUM * moment + grad
    weight_new = weight - rate * (grad + MOMENTUM * moment_new)
    average_new = AVG_DECAY * average + (1.0 - AVG_DECAY) * weight_new
    return moment_new, weight_new, average_new


def update_kernel(rate_scale, gsum_hbm, nsum_hbm, tlow_hbm, bout_hbm, *refs):
    sources, targets = refs[0:15], refs[15:37]
    gsum, nsum, tlow, bout, tgrad, *held, in_sems, out_sems = refs[37:]
    fetched, results = held[0:15], held[15:35]
    moves = (
        (tlow_hbm, tlow), (bout_hbm, bout), (gsum_hbm, gsum), (nsum_hbm, nsum),
        *zip(sources, fetched),
    )
    fetches = [
        pltpu.make_async_copy(src, dst, in_sems.at[number])
        for number, (src, dst) in enumerate(moves)
    ]
    for fetch in fetches:
        fetch.start()
    stores = []

    def store(src, number):
        copy = pltpu.make_async_copy(src, targets[number], out_sems.at[number])
        copy.start()
        stores.append(copy)

    fetches[0].wait()
    tgrad[...] = tlow[...].astype(F32)
    store(tgrad, 1)
    fetches[1].wait()
    store(bout, 0)
    fetches[2].wait()
    fetches[3].wait()
    for which in range(5):
        weight, moment, average = fetched[which], fetched[5 + which], fetched[10 + which]
        for turn in range(3):
            fetches[4 + 5 * turn + which].wait()
        if which < 4:
            parts = [
                ((index,) if which < 2 else (slice(None), slice(index * 128, index * 128 + 128)), gsum[block])
                for block, (array, index) in enumerate(BLOCK_OF)
                if array == which
            ]
        else:
            parts = [((slice(None), slice(None)), nsum[0:6, 0 : weight.shape[1]])]
        for at, grad in parts:
            rate = BASE_RATES[which] * rate_scale
            found = update(weight[at], grad, moment[at], average[at], rate)
            for number, value in enumerate((grad, *found)):
                results[4 * which + number][at] = value
        for number in range(4):
            store(results[4 * which + number], 2 + 4 * which + number)
    for copy in stores:
        copy.wait()


def per_device(nz, *args):
    (tokens, memory, cotangent, lengths, breaks, attn_in, attn_out, ffn_in, ffn_out, norms) = args[:10]
    moments, averages = args[10:15], args[15:20]
    own = attn_in.shape[1]
    whole = (nz, 2, own, 128)
    smem = pl.BlockSpec(memory_space=pltpu.SMEM)
    hbm = pl.BlockSpec(memory_space=pl.ANY)
    dma = pltpu.SemaphoreType.DMA

    def bf(*shape):
        return pltpu.VMEM(shape, BF)

    def f32(*shape):
        return pltpu.VMEM(shape, F32)

    def landing(parcel, phase):
        _, count, route = parcel
        sizes = {"x": 2, "y": 2, "z": nz}
        left = [axis for axis in "xyz" if axis not in route[: phase + 1]]
        senders = nz - 1 if route[phase] == "z" else 1
        sides = [2] if "x" in left else []
        rest = [sizes[axis] for axis in "zy" if axis in left]
        return bf(senders, *sides, count, *rest, own, 128)

    landings = [[landing(parcel, phase) for phase in range(3)] for parcel in SUM]
    scratch = [
        f32(BLOCKS, own, 128), f32(8, 128), bf(2, SEQ, WIDTH), bf(2, SEQ, WIDTH),
        *[f32(*array.shape) for array in (attn_in, attn_out, ffn_in, ffn_out, norms)],
        bf(SEQ, WIDTH), bf(SEQ, WIDTH), bf(SEQ, WIDTH),
        bf(2, BLOCKS, *whole), bf(2, BLOCKS, *whole),
        landings,
        f32(nz, 2, 8, 128), f32(8, 128), f32(8, WIDTH),
        f32(6, 8, WIDTH), f32(2, 8, WIDTH), f32(2, 8, WIDTH), f32(nz, 8, WIDTH),
        f32(8, WIDTH),
        bf(6, SEQ, WIDTH), bf(6, SEQ, WIDTH),
        f32(SEQ, WIDTH), f32(3, SEQ, WIDTH), f32(3, SEQ, 1),
        f32(SEQ, WIDTH), f32(SEQ, WIDTH),
        bf(3, SEQ, WIDTH), bf(5, WIDTH, SEQ),
        bf(2, SEQ, COLS), bf(2, SEQ, COLS), bf(2, SEQ, COLS),
        bf(2, HEADS_HERE, SEQ, COLS), bf(2, HEADS_HERE, SEQ, COLS),
        bf(2, HEADS_HERE, SEQ, SEQ), bf(HEADS_HERE, SEQ, SEQ),
        bf(2, SEQ, COLS), f32(SEQ, WIDTH),
        bf(SEQ, COLS), bf(SEQ, COLS), bf(SEQ, COLS),
        bf(SEQ, COLS), bf(SEQ, COLS), bf(SEQ, WIDTH), bf(SEQ, COLS), bf(COLS, SEQ),
        dma((12,)), dma((len(GATHER),)), dma((len(GATHER), 3)),
        dma((len(GATHER),)),
        dma((len(SUM),)), dma((len(SUM), 3)),
        dma((nz,)), dma((nz,)),
        dma((6, 2)), dma((6, 2)),
        dma((nz + 1,)), dma((nz + 1,)), dma((2, 2)), dma((2, 2)),
    ]
    gsum, nsum, bout, tlow = pl.pallas_call(
        functools.partial(layer_kernel, nz),
        out_shape=(
            jax.ShapeDtypeStruct((BLOCKS, own, 128), F32),
            jax.ShapeDtypeStruct((8, 128), F32),
            jax.ShapeDtypeStruct((2, SEQ, WIDTH), BF),
            jax.ShapeDtypeStruct((2, SEQ, WIDTH), BF),
        ),
        in_specs=[hbm] * 3 + [smem] * 2 + [hbm] * 5,
        out_specs=(hbm,) * 4,
        scratch_shapes=scratch,
        compiler_params=pltpu.CompilerParams(
            collective_id=0, has_side_effects=True, vmem_limit_bytes=58 * 2**20
        ),
    )(tokens, memory, cotangent, lengths, breaks, attn_in, attn_out, ffn_in, ffn_out, norms)
    weights = (attn_in, attn_out, ffn_in, ffn_out, norms)
    rate_scale = float(lax.axis_size("dp") * tokens.shape[0]) ** -0.5
    results = pl.pallas_call(
        functools.partial(update_kernel, rate_scale),
        out_shape=(
            jax.ShapeDtypeStruct((2, SEQ, WIDTH), BF),
            jax.ShapeDtypeStruct((2, SEQ, WIDTH), F32),
            *[jax.ShapeDtypeStruct(w.shape, F32) for w in weights for _ in range(4)],
        ),
        in_specs=[hbm] * 19,
        out_specs=(hbm,) * 22,
        scratch_shapes=[
            f32(BLOCKS, own, 128), f32(8, 128), bf(2, SEQ, WIDTH), bf(2, SEQ, WIDTH), f32(2, SEQ, WIDTH),
            *[f32(*w.shape) for w in (*weights, *moments, *averages)],
            *[f32(*w.shape) for w in weights for _ in range(4)],
            dma((19,)), dma((22,)),
        ],
        compiler_params=pltpu.CompilerParams(vmem_limit_bytes=63 * 2**20),
    )(gsum, nsum, tlow, bout, *weights, *moments, *averages)
    return (results[0].reshape(tokens.shape), results[1].reshape(tokens.shape), *results[2:])


def solution(mesh):
    rows, attn, ffn, norm = P("dp", None), P(None, "dp", "tensor"), P("dp", "tensor"), P(None, "dp")
    weights = (attn, attn, ffn, ffn, norm)
    return jax.shard_map(
        functools.partial(per_device, mesh.shape["dp"] // 2),
        mesh=mesh,
        in_specs=(rows, rows, rows, P("dp"), P("dp")) + weights * 3,
        out_specs=(rows, rows) + tuple(spec for spec in weights for _ in range(4)),
        check_vma=False,
    )
```
